32 devices in a mesh: shot: 2 (over y), gx: 4 (over z), gy: 4 (over x, core).
Axes of the slice: x: 2, y: 2, z: 4, core: 2. Of those that a mesh axis runs over, the one named last changes fastest.
Arguments:
- source_prev: float32 [64, 32, 320], P(('shot', 'gx'), 'gy'), parts along dimension 0, may hold values from -0.6 to 0.6
- source_now: float32 [64, 32, 320], P(('shot', 'gx'), 'gy'), parts along dimension 0, may hold values from -0.6 to 0.6
- receiver_prev: float32 [64, 32, 320], P(('shot', 'gx'), 'gy'), parts along dimension 0, may hold values from -6 to 6
- receiver_now: float32 [64, 32, 320], P(('shot', 'gx'), 'gy'), parts along dimension 0, may hold values from -6 to 6
- speed_squared: float32 [64, 32, 320], P(('shot', 'gx'), 'gy'), parts along dimension 0, may hold values from 0.05 to 0.18
- wavelet: float32 [20], P('shot'), parts along dimension 0, may hold values from -40 to 40
- source_cell: int32 [2], P('shot'), parts along dimension 0, may hold values from 0 to 327679
- traces: float32 [20, 1024], P('shot', ('gx', 'gy')), parts along dimension 0, may hold values from -18 to 18
- receiver_cells: int32 [2, 1024], P('shot', ('gx', 'gy')), parts along dimension 0, may hold values from 0 to 1023
- plan: int32 [8], P('shot'), parts along dimension 0, may hold values from 0 to 9, as said below
- stored_snapshots: bfloat16 [8, 32, 32, 320], P('shot', 'gx', 'gy'), parts along dimension 0, may hold values from -6 to 6
- image_before: float32 [64, 32, 320], P(('shot', 'gx'), 'gy'), parts along dimension 0, may hold values from -6 to 6
Outputs:
- new_source_prev: float32 [64, 32, 320], P(('shot', 'gx'), 'gy'), parts along dimension 0
- new_source_now: float32 [64, 32, 320], P(('shot', 'gx'), 'gy'), parts along dimension 0
- new_receiver_prev: float32 [64, 32, 320], P(('shot', 'gx'), 'gy'), parts along dimension 0
- new_receiver_now: float32 [64, 32, 320], P(('shot', 'gx'), 'gy'), parts along dimension 0
- snapshots: bfloat16 [8, 32, 32, 320], P('shot', 'gx', 'gy'), parts along dimension 0
- image: float32 [64, 32, 320], P(('shot', 'gx'), 'gy'), parts along dimension 0
The draws below stay inside these ranges and needn't reach their ends.
There are 2 independent parts, one for each index of `shot`. The reference program is written for one: setup_inputs(seed, part) draws one part's arguments, and reference() takes and returns one part's arrays. A program takes and returns all parts, laid end to end along the dimension named above; each array names one. Nothing has to cross between parts.
Inputs may be any that keep to these rules, and one draw needn't show every extreme that they name: `plan`: 4 different steps in increasing order; the first is 0 and the last is 9.
All inputs are finite; a program needn't handle non-finite values.
Results may differ from the reference program's by a relative error of at most 0.001.
Values sent between devices are 32-bit elements; how exact they have to be, the bound alone decides.
No kernel may reach another device: no remote copies, remote signals or barrier semaphores. Data moves between devices by JAX's collectives and lax.ppermute only.
A program may use at most 64 MiB of HBM per device.

```python
import math
import jax
import jax.numpy as jnp
from jax import lax

NZ = 320
STEPS = 10
NSNAP = 4
NX = 32
NY = 32
NREC = 1024


def draw_plan(key, part):
    middle = jax.random.permutation(jax.random.fold_in(key, 11), STEPS - 2)[:NSNAP - 2] + 1
    middle = jnp.sort(middle.astype(jnp.int32))
    return jnp.concatenate([jnp.zeros((1,), jnp.int32), middle, jnp.full((1,), STEPS - 1, jnp.int32)])


def touch_ends(values, stream_key, least, largest):
    longest = values.shape.index(max(values.shape))
    spots = []
    for shift in (0, 1):
        where = [jax.random.randint(jax.random.fold_in(stream_key, axis), (), 0, length) for axis, length in enumerate(values.shape)]
        where[longest] = (where[longest] + shift) % values.shape[longest]
        spots.append(tuple(where))
    return values.at[spots[0]].set(least).at[spots[1]].set(largest)


def level_of(rng, shape, shards, low, high):
    level = 1.0
    for dim, blocks in shards:
        heights = jax.random.uniform(jax.random.fold_in(jax.random.fold_in(rng, 6), dim), (blocks,), jnp.float32, low / len(shards), high / len(shards))
        level = level * jnp.repeat(jnp.exp(heights), shape[dim] // blocks).reshape((-1,) + (1,) * (len(shape) - 1 - dim))
    return level


def normal_values(own_key, shape, deviation, most, cuts=(), kind=jnp.bfloat16):
    drawn = deviation * jax.random.normal(own_key, shape, jnp.float32)
    if cuts:
        drawn = drawn * level_of(own_key, shape, cuts, -0.22, 0.18)
    return jnp.clip(drawn, -most, most).astype(kind)


def setup_inputs(seed: int = 0, part: int = 0) -> dict:
    arg_keys = jax.random.split(jax.random.key(seed), 13)
    part_keys = jax.random.split(jax.random.fold_in(arg_keys[12], part), 13)
    source_prev = normal_values(part_keys[0], (NX, NY, NZ), 0.1, 0.6, ((0, 4), (1, 4)), jnp.float32)
    source_now = normal_values(part_keys[1], (NX, NY, NZ), 0.1, 0.6, ((0, 4), (1, 4)), jnp.float32)
    receiver_prev = normal_values(part_keys[2], (NX, NY, NZ), 1.0, 6.0, ((0, 4), (1, 4)), jnp.float32)
    receiver_now = normal_values(part_keys[3], (NX, NY, NZ), 1.0, 6.0, ((0, 4), (1, 4)), jnp.float32)
    speed_squared = jnp.clip(jnp.exp(math.log(0.18) - 1.2809339 * jax.random.uniform(part_keys[4], (NX, NY, NZ), jnp.float32) ** level_of(part_keys[4], (NX, NY, NZ), ((0, 4), (1, 4)), -0.2, 0.2)), 0.05, 0.18)
    wavelet = normal_values(part_keys[5], (STEPS,), 8.0, 40.0, (), jnp.float32)
    source_cell = jax.random.randint(part_keys[6], (1,), 0, NX * NY * NZ).astype(jnp.int32)
    traces = normal_values(part_keys[7], (STEPS, NREC), 3.0, 18.0, ((1, 16),), jnp.float32)
    receiver_cells = touch_ends(jax.random.randint(part_keys[8], (1, NREC), 0, NX * NY), jax.random.fold_in(part_keys[8], 1), 0, (NX * NY) - 1).astype(jnp.int32)
    plan = draw_plan(jax.random.fold_in(jax.random.fold_in(arg_keys[12], part), 71), part)
    stored_snapshots = normal_values(part_keys[10], (NSNAP, NX, NY, NZ), 1.0, 6.0, ((1, 4), (2, 4)))
    image_before = normal_values(part_keys[11], (NX, NY, NZ), 1.0, 6.0, ((0, 4), (1, 4)), jnp.float32)
    return {"source_prev": source_prev, "source_now": source_now, "receiver_prev": receiver_prev, "receiver_now": receiver_now, "speed_squared": speed_squared, "wavelet": wavelet, "source_cell": source_cell, "traces": traces, "receiver_cells": receiver_cells, "plan": plan, "stored_snapshots": stored_snapshots, "image_before": image_before}


STENCIL_COEFFS = (-205.0 / 72.0, 8.0 / 5.0, -1.0 / 5.0, 8.0 / 315.0, -1.0 / 560.0)


def stencil(padded):
    span_x = padded.shape[0] - 8
    span_y = padded.shape[1] - 8
    depth_cells = padded.shape[2]
    deepened = jnp.pad(padded, ((0, 0), (0, 0), (4, 4)))

    def window(shift_x, shift_y, shift_z):
        return deepened[4 + shift_x:4 + shift_x + span_x, 4 + shift_y:4 + shift_y + span_y,
                        4 + shift_z:4 + shift_z + depth_cells]

    summed = (3.0 * STENCIL_COEFFS[0]) * window(0, 0, 0)
    for distance in range(1, 5):
        neighbours = window(distance, 0, 0) + window(-distance, 0, 0)
        neighbours = neighbours + window(0, distance, 0) + window(0, -distance, 0)
        neighbours = neighbours + window(0, 0, distance) + window(0, 0, -distance)
        summed = summed + STENCIL_COEFFS[distance] * neighbours
    return summed


def reference(source_prev, source_now, receiver_prev, receiver_now, speed_squared, wavelet,
              source_cell, traces, receiver_cells, plan, stored_snapshots, image_before):
    grid_x, grid_y, depth_cells = source_now.shape
    total_steps = wavelet.shape[0]
    slot_count = plan.shape[0]
    cell_id = source_cell[0]
    site_x = cell_id // (grid_y * depth_cells)
    site_y = (cell_id // depth_cells) % grid_y
    site_z = cell_id % depth_cells
    previous, current = source_prev, source_now
    snapshots = jnp.zeros(stored_snapshots.shape, jnp.bfloat16)
    for step_index in range(total_steps):
        spread = stencil(jnp.pad(current, ((4, 4), (4, 4), (0, 0))))
        spread = spread.at[site_x, site_y, site_z].add(wavelet[step_index])
        latest = 2.0 * current - previous + speed_squared * spread
        previous, current = current, latest
        matches = plan == step_index
        snapshots = jnp.where(matches[:, None, None, None], current.astype(jnp.bfloat16)[None], snapshots)
    source_last, source_final = previous, current

    planes = jnp.zeros((total_steps, grid_x * grid_y), jnp.float32).at[:, receiver_cells[0]].add(traces)
    planes = planes.reshape(total_steps, grid_x, grid_y)
    previous, current = receiver_prev, receiver_now
    imaged = image_before
    for step_index in range(total_steps):
        back_time = total_steps - 1 - step_index
        spread = stencil(jnp.pad(current, ((4, 4), (4, 4), (0, 0))))
        spread = spread.at[:, :, 0].add(planes[back_time])
        latest = 2.0 * current - previous + speed_squared * spread
        previous, current = current, latest
        matches = plan == back_time
        slot_index = jnp.sum(jnp.where(matches, jnp.arange(slot_count, dtype=jnp.int32), 0)).astype(jnp.int32)
        present = jnp.any(matches)
        snapshot = lax.dynamic_index_in_dim(stored_snapshots, slot_index, 0, keepdims=False).astype(jnp.float32)
        imaged = imaged + jnp.where(present, snapshot * current, 0.0)
    return (source_last, source_final, previous, current, snapshots, imaged)
```

```python
import functools

import jax
import jax.numpy as jnp
from jax import lax
from jax.experimental import pallas as pl
from jax.experimental.pallas import tpu as pltpu
from jax.sharding import PartitionSpec as P

STENCIL_COEFFS = (-205.0 / 72.0, 8.0 / 5.0, -1.0 / 5.0, 8.0 / 315.0, -1.0 / 560.0)
REACH = 4
HALO = 2 * REACH
LANES = 128
ROWS = 8
AXES = ("gx", "gy")


class Layout:
    def __init__(self, mesh, block_x, block_y, depth, steps, slots):
        self.nx, self.ny = mesh.shape["gx"], mesh.shape["gy"]
        self.columns = self.ny // 2
        self.bx, self.by, self.depth = block_x, block_y, depth
        self.steps, self.slots = steps, slots
        self.cy = 2 * block_y
        self.zt = pl.cdiv(depth + REACH, LANES)
        self.rest = depth - (self.zt - 1) * LANES
        self.packed = 0 < self.rest <= LANES // 2
        self.ex, self.ey = block_x + 2 * REACH, self.cy + 2 * REACH
        self.zrows = self.cy * (self.zt - 1) + self.cy // 2 if self.packed else self.cy * self.zt
        self.z_parities = [p for p in (0, 1) if p + 1 < self.nx]
        self.y_parities = [p for p in (0, 1) if p + 1 < self.columns]
        assert self.ny % 2 == 0 and block_x >= HALO and block_y % ROWS == 0 and steps % 2 == 0

    def device(self, x, column, core):
        return x * self.ny + 2 * column + core

    def permutation(self, move):
        pairs = []
        for x in range(self.nx):
            for column in range(self.columns):
                other = move(x, column)
                there = 0 <= other[0] < self.nx and 0 <= other[1] < self.columns
                for core in (0, 1):
                    target = self.device(*other, core) if there else self.device(x, column, 1 - core)
                    pairs.append((self.device(x, column, core), target))
        return pairs

    def z_permutation(self, pz):
        return self.permutation(lambda x, c: (x + (1 if x % 2 == pz else -1), c))

    def y_permutation(self, py):
        return self.permutation(lambda x, c: (x, c + (1 if c % 2 == py else -1)))

    def d_permutation(self, pz, py):
        return self.permutation(
            lambda x, c: (x + (1 if x % 2 == pz else -1), c + (1 if c % 2 == py else -1))
        )

    def core_permutation(self):
        return self.permutation(lambda x, c: (-1, -1))

    def place(self):
        gx, gy = lax.axis_index("gx"), lax.axis_index("gy")
        return gx, gy // 2, gy % 2

    def z_side(self, pz):
        gx, _, _ = self.place()
        right = gx % 2 == pz
        return right, jnp.where(right, gx + 1 < self.nx, gx > 0)

    def y_side(self, py):
        _, column, _ = self.place()
        high = column % 2 == py
        return high, jnp.where(high, column + 1 < self.columns, column > 0)


def lane_ids(rows):
    return lax.broadcasted_iota(jnp.int32, (rows, LANES), 1)


def pack(tiles, lay, rows):
    if not lay.packed:
        return list(tiles)
    last = tiles[-1]
    return list(tiles[:-1]) + [last[: rows // 2] + pltpu.roll(last[rows // 2 :], LANES // 2, 1)]


def unpack(block, lay, rows):
    tiles = [block[t * rows : (t + 1) * rows] for t in range(lay.zt - 1)]
    start = (lay.zt - 1) * rows
    if not lay.packed:
        return tiles + [block[start : start + rows]]
    both = block[start : start + rows // 2]
    low = lane_ids(rows // 2) < LANES // 2
    first = jnp.where(low, both, 0.0)
    second = pltpu.roll(jnp.where(low, 0.0, both), LANES // 2, 1)
    return tiles + [jnp.concatenate([first, second], 0)]


def store_packed(ref, index, tiles, lay, rows):
    row = 0
    for piece in pack(tiles, lay, rows):
        ref[index, row : row + piece.shape[0], :] = piece
        row += piece.shape[0]


def write_y_message(ref, lead, source, lay, high):
    for x in range(lay.bx):
        for t in range(lay.zt):
            rows = jnp.where(
                high, source[x, t, lay.cy - ROWS : lay.cy, :], source[x, t, 0:ROWS, :]
            )
            ref[lead * lay.bx + x, t * ROWS : (t + 1) * ROWS, :] = rows


def write_d_message(ref, source, lay, right, high):
    start = jnp.where(right, lay.bx - REACH, 0)
    for x in range(REACH):
        for t in range(lay.zt):
            rows = jnp.where(
                high,
                source[start + x, t, lay.cy - ROWS : lay.cy, :],
                source[start + x, t, 0:ROWS, :],
            )
            ref[x, t * ROWS : (t + 1) * ROWS, :] = rows


def prepare_kernel(lay, *refs):
    (src_now, src_prev, rec_now, rec_prev, speed, other), refs = refs[:6], refs[6:]
    (p, q, s), refs = refs[:3], refs[3:]
    nz, ny = len(lay.z_parities), len(lay.y_parities)
    z_messages, refs = refs[:nz], refs[nz:]
    y_messages, d_messages = refs[:ny], refs[ny:]
    _, _, core = lay.place()
    first = core == 0
    edge = (lay.zt - 1) * LANES
    for ref in (p, q, s):
        ref[:, lay.zt - 1, :, :] = jnp.zeros((lay.bx, lay.cy, LANES), jnp.float32)
    for index, (ref, a, b) in enumerate(((p, src_now, rec_now), (q, src_prev, rec_prev), (s, speed, speed))):
        for x in range(lay.bx):
            for t in range(lay.zt):
                width = LANES if t + 1 < lay.zt else lay.rest
                lanes = slice(t * LANES, t * LANES + width)
                mine = a[x, :, lanes] if a is b else jnp.where(first, a[x, :, lanes], b[x, :, lanes])
                theirs = other[index, x, :, lanes]
                ref[x, t, 0 : lay.by, 0:width] = jnp.where(first, mine, theirs)
                ref[x, t, lay.by : lay.cy, 0:width] = jnp.where(first, theirs, mine)
    sides = [lay.z_side(pz)[0] for pz in lay.z_parities]
    for x in range(lay.bx):
        tiles = [p[x, t] for t in range(lay.zt)]
        for message in z_messages:
            store_packed(message, x, tiles, lay, lay.cy)
    for message, right in zip(z_messages, sides):
        start = jnp.where(right, lay.bx - REACH, 0)
        for lead, ref in ((0, q), (1, s)):
            for x in range(REACH):
                tiles = [ref[start + x, t] for t in range(lay.zt)]
                store_packed(message, lay.bx + lead * REACH + x, tiles, lay, lay.cy)
    highs = [lay.y_side(py)[0] for py in lay.y_parities]
    for message, high in zip(y_messages, highs):
        for lead, ref in enumerate((p, q, s)):
            write_y_message(message, lead, ref, lay, high)
    corners = [(right, high) for right in sides for high in highs]
    for message, (right, high) in zip(d_messages, corners):
        write_d_message(message, p, lay, right, high)


def planes_kernel(lay, gathered, planes, total):
    gx, column, core = lay.place()
    start_x, start_y = gx * lay.bx - REACH, column * lay.cy - REACH
    cells = lay.ex * lay.ey
    padded = gathered.shape[1]
    total[...] = jnp.zeros_like(total)

    def add(index, carry):
        values = gathered[index]
        x = values[lay.steps : lay.steps + 1, :].astype(jnp.int32) - start_x
        y = values[lay.steps + 1 : lay.steps + 2, :].astype(jnp.int32) - start_y
        inside = (x >= 0) & (x < lay.ex) & (y >= 0) & (y < lay.ey)
        cell = jnp.where(inside, x * lay.ey + y, -1)
        ids = lax.broadcasted_iota(jnp.int32, (cells, LANES), 0)
        chosen = jnp.where(ids == cell, 1.0, 0.0).astype(jnp.bfloat16)
        high = values.astype(jnp.bfloat16)
        rest = values - high.astype(jnp.float32)
        middle = rest.astype(jnp.bfloat16)
        low = (rest - middle.astype(jnp.float32)).astype(jnp.bfloat16)
        fill = jnp.zeros((LANES - 3 * padded, LANES), jnp.bfloat16)
        parts = jnp.concatenate([high, middle, low, fill], 0)
        total[...] += lax.dot_general(
            chosen, parts, (((1,), (1,)), ((), ())), preferred_element_type=jnp.float32
        )
        return carry

    lax.fori_loop(0, gathered.shape[0], add, 0)
    summed = total[...]
    summed = (
        summed + pltpu.roll(summed, LANES - padded, 1) + pltpu.roll(summed, LANES - 2 * padded, 1)
    )
    summed = jnp.where(core == 1, summed, 0.0)
    planes[...] = summed.reshape(lay.ex, lay.ey, LANES)


def advance(lay, field, x, y, rows, before, speed, injected):
    lane = lane_ids(rows)
    centre = [field[x, t, y : y + rows, :] for t in range(lay.zt)]
    sums = []
    for k in range(1, REACH + 1):
        left = [pltpu.roll(c, k, 1) for c in centre]
        right = [pltpu.roll(c, LANES - k, 1) for c in centre]
        per_tile = []
        for t in range(lay.zt):
            lower = jnp.where(lane < k, left[t - 1], left[t])
            upper = jnp.where(lane < LANES - k, right[t], right[(t + 1) % lay.zt])
            around = field[x - k, t, y : y + rows, :] + field[x + k, t, y : y + rows, :]
            around += field[x, t, y - k : y - k + rows, :] + field[x, t, y + k : y + k + rows, :]
            per_tile.append(around + (lower + upper))
        sums.append(per_tile)
    out = []
    for t in range(lay.zt):
        drive = 3.0 * STENCIL_COEFFS[0] * centre[t]
        for k in range(REACH):
            drive += STENCIL_COEFFS[k + 1] * sums[k][t]
        if t == 0:
            drive += injected
        out.append(2.0 * centre[t] - before[t] + speed[t] * drive)
    return out


def round_kernel(lay, time, first, last, *refs):
    nz, ny = len(lay.z_parities), len(lay.y_parities)
    (wavelet, where, p, q, s, planes), refs = refs[:6], refs[6:]
    z_in, refs = refs[:nz], refs[nz:]
    y_in, refs = refs[:ny], refs[ny:]
    d_in, refs = refs[: nz * ny], refs[nz * ny :]
    (middle, latest), refs = refs[:2], refs[2:]
    if last:
        q_out, buffer = refs[:2]
    else:
        (q_out, z_out), refs = refs[:2], refs[2:]
        y_out, refs = refs[:ny], refs[ny:]
        d_out, refs = refs[: nz * ny], refs[nz * ny :]
        if first:
            s_out, q_ext, buffer = refs
        else:
            (buffer,) = refs
    z_sides = [lay.z_side(pz) for pz in lay.z_parities]
    y_sides = [lay.y_side(py) for py in lay.y_parities]
    bx, cy, zt = lay.bx, lay.cy, lay.zt
    own_x, own_y = HALO, HALO

    buffer[own_x : own_x + bx, :, own_y : own_y + cy, :] = p[...]
    for is_right, start in ((False, 0), (True, own_x + bx)):
        wants = [v & (r if is_right else ~r) for r, v in z_sides]
        for x in range(HALO):
            row = x if is_right else bx - HALO + x
            block = sum((jnp.where(w, m[row], 0.0) for w, m in zip(wants, z_in)), jnp.zeros((lay.zrows, LANES), jnp.float32))
            for t, tile in enumerate(unpack(block, lay, cy)):
                buffer[start + x, t, own_y : own_y + cy, :] = tile
    for is_high, start in ((False, 0), (True, own_y + cy)):
        wants = [v & (h if is_high else ~h) for h, v in y_sides]
        for x in range(bx):
            for t in range(zt):
                rows = slice(t * ROWS, (t + 1) * ROWS)
                buffer[own_x + x, t, start : start + ROWS, :] = sum(
                    (jnp.where(w, m[x, rows, :], 0.0) for w, m in zip(wants, y_in)),
                    jnp.zeros((ROWS, LANES), jnp.float32),
                )
        for is_right, x_start in ((False, own_x - REACH), (True, own_x + bx)):
            corner = [
                v & u & (r if is_right else ~r) & (h if is_high else ~h)
                for r, v in z_sides
                for h, u in y_sides
            ]
            for x in range(REACH):
                for t in range(zt):
                    rows = slice(t * ROWS, (t + 1) * ROWS)
                    buffer[x_start + x, t, start : start + ROWS, :] = sum(
                        (jnp.where(w, m[x, rows, :], 0.0) for w, m in zip(corner, d_in)),
                        jnp.zeros((ROWS, LANES), jnp.float32),
                    )

    if first:
        for lead, own, ext in ((0, q, q_ext), (1, s, s_out)):
            ext[...] = jnp.zeros_like(ext)
            for x in range(bx):
                for t in range(zt):
                    ext[REACH + x, t, REACH : REACH + cy, :] = own[x, t]
            for is_right, start in ((False, 0), (True, REACH + bx)):
                wants = [v & (r if is_right else ~r) for r, v in z_sides]
                for x in range(REACH):
                    row = bx + lead * REACH + x
                    block = sum((jnp.where(w, m[row], 0.0) for w, m in zip(wants, z_in)), jnp.zeros((lay.zrows, LANES), jnp.float32))
                    for t, tile in enumerate(unpack(block, lay, cy)):
                        ext[start + x, t, REACH : REACH + cy, :] = tile
            for is_high, start, cut in ((False, 0, ROWS - REACH), (True, REACH + cy, 0)):
                wants = [v & (h if is_high else ~h) for h, v in y_sides]
                for x in range(bx):
                    for t in range(zt):
                        rows = slice(t * ROWS + cut, t * ROWS + cut + REACH)
                        ext[REACH + x, t, start : start + REACH, :] = sum(
                            (jnp.where(w, m[(lead + 1) * bx + x, rows, :], 0.0) for w, m in zip(wants, y_in)),
                            jnp.zeros((REACH, LANES), jnp.float32),
                        )
        q, s = q_ext, s_out

    def injected(x, rows, y, back):
        values = pltpu.roll(planes[x], LANES - back, 1) if back else planes[x]
        return jnp.where(lane_ids(lay.ey) == 0, values, 0.0)[y : y + rows]

    def add_source(target, speed_rows, x, y, count_x, count_y, amount):
        @pl.when((x >= 0) & (x < count_x) & (y >= 0) & (y < count_y))
        def _():
            depth = where[2]
            tile, lane = depth // LANES, depth % LANES
            shape = (count_y, LANES)
            here = (lax.broadcasted_iota(jnp.int32, shape, 0) == y) & (
                lax.broadcasted_iota(jnp.int32, shape, 1) == lane
            )
            target[x, tile] += jnp.where(here, speed_rows(x, tile) * amount, 0.0)

    def step_one(x, carry):
        out = advance(
            lay, buffer, x + REACH, REACH, lay.ey,
            [q[x, t] for t in range(zt)], [s[x, t] for t in range(zt)],
            injected(x, lay.ey, 0, lay.steps - 1 - time),
        )
        for t in range(zt):
            q_out[x, t] = out[t]
        return carry

    lax.fori_loop(0, lay.ex, step_one, 0)
    add_source(q_out, lambda x, t: s[x, t], where[0] + REACH, where[1] + REACH, lay.ex, lay.ey, wavelet[time])

    def step_two(x, carry):
        out = advance(
            lay, q_out, x + REACH, REACH, cy,
            [p[x, t] for t in range(zt)],
            [s[x + REACH, t, REACH : REACH + cy, :] for t in range(zt)],
            injected(x + REACH, cy, REACH, lay.steps - 2 - time),
        )
        for t in range(zt):
            latest[x, t] = out[t]
            middle[x, t] = q_out[x + REACH, t, REACH : REACH + cy, :]
        return carry

    lax.fori_loop(0, bx, step_two, 0)
    add_source(
        latest, lambda x, t: s[x + REACH, t, REACH : REACH + cy, :], where[0], where[1], bx, cy, wavelet[time + 1]
    )

    if not last:
        for x in range(bx):
            store_packed(z_out, x, [latest[x, t] for t in range(zt)], lay, cy)
        for message, (high, _) in zip(y_out, y_sides):
            write_y_message(message, 0, latest, lay, high)
        corners = [(right, high) for right, _ in z_sides for high, _ in y_sides]
        for message, (right, high) in zip(d_out, corners):
            write_d_message(message, latest, lay, right, high)


def collect_kernel(lay, times, *refs):
    fields, own, theirs = refs[: lay.steps], refs[lay.steps], refs[lay.steps + 1]
    _, _, core = lay.place()

    def put(index, field):
        for x in range(lay.bx):
            for t in range(lay.zt):
                low, high = field[x, t, 0 : lay.by, :], field[x, t, lay.by : lay.cy, :]
                own[index, x, t] = jnp.where(core == 0, low, high)
                theirs[index, x, t] = jnp.where(core == 0, high, low)

    put(0, fields[lay.steps - 2])
    put(1, fields[lay.steps - 1])
    for slot in range(lay.slots - 1):
        for time in range(lay.steps):
            pl.when(times[slot] == time)(functools.partial(put, 2 + slot, fields[time]))


def finish_kernel(lay, own, theirs, stored, image_before, *outs):
    src_prev, src_now, rec_prev, rec_now, snapshots, image = outs
    _, _, core = lay.place()
    first = core == 0
    for x in range(lay.bx):
        for t in range(lay.zt):
            width = LANES if t + 1 < lay.zt else lay.rest
            lanes = slice(t * LANES, t * LANES + width)
            source = [jnp.where(first, own[i, x, t], theirs[i, x, t])[:, :width] for i in range(lay.slots + 1)]
            receiver = [jnp.where(first, theirs[i, x, t], own[i, x, t])[:, :width] for i in range(lay.slots + 1)]
            src_prev[x, :, lanes], src_now[x, :, lanes] = source[0], source[1]
            rec_prev[x, :, lanes], rec_now[x, :, lanes] = receiver[0], receiver[1]
            total = image_before[x, :, lanes]
            for slot in range(lay.slots):
                kept = source[1] if slot == lay.slots - 1 else source[2 + slot]
                snapshots[slot, x, :, lanes] = kept.astype(jnp.bfloat16)
                crossed = receiver[1] if slot == 0 else receiver[1 + lay.slots - slot]
                total += stored[slot, x, :, lanes].astype(jnp.float32) * crossed
            image[x, :, lanes] = total


def call(kernel, outs, operands, scratch=(), scalars=0):
    in_specs = [pl.BlockSpec(memory_space=pltpu.SMEM)] * scalars
    in_specs += [pl.BlockSpec(memory_space=pltpu.VMEM)] * (len(operands) - scalars)
    return pl.pallas_call(
        kernel,
        out_shape=[jax.ShapeDtypeStruct(shape, dtype) for shape, dtype in outs],
        in_specs=in_specs,
        out_specs=[pl.BlockSpec(memory_space=pltpu.VMEM)] * len(outs),
        scratch_shapes=list(scratch),
        compiler_params=pltpu.CompilerParams(vmem_limit_bytes=16 * 1024 * 1024),
    )(*operands)


def gather_traces(lay, traces, receiver_cells):
    grid_y = lay.by * lay.ny
    cells = receiver_cells
    rows = [traces, (cells // grid_y).astype(jnp.float32), (cells % grid_y).astype(jnp.float32)]
    padded = pl.cdiv(lay.steps + 2, 2 * ROWS) * 2 * ROWS
    rows.append(jnp.zeros((padded - lay.steps - 2, traces.shape[1]), jnp.float32))
    message = jnp.concatenate(rows, 0)
    other = lax.ppermute(message, AXES, lay.core_permutation())
    message = jnp.concatenate([message, other], 1)[None]
    if message.shape[2] != LANES:
        spare = -message.shape[2] % LANES
        fill = jnp.full((1, padded, spare), -1e6, jnp.float32)
        message = jnp.concatenate([message, fill], 2)
        message = message.reshape(padded, -1, LANES).transpose(1, 0, 2)
    for count, move in (
        (lay.columns, lambda x, c, bit: (x, c ^ bit)),
        (lay.nx, lambda x, c, bit: (x ^ bit, c)),
    ):
        assert count & (count - 1) == 0
        bit = 1
        while bit < count:
            pairs = lay.permutation(functools.partial(move, bit=bit))
            message = jnp.concatenate([message, lax.ppermute(message, AXES, pairs)], 0)
            bit *= 2
    return message


def body(
    mesh,
    source_prev,
    source_now,
    receiver_prev,
    receiver_now,
    speed_squared,
    wavelet,
    source_cell,
    traces,
    receiver_cells,
    plan,
    stored_snapshots,
    image_before,
):
    steps, slots = wavelet.shape[0], plan.shape[0]
    lay = Layout(mesh, *source_now.shape, steps, slots)
    f32 = jnp.float32
    gx, gy = lax.axis_index("gx"), lax.axis_index("gy")
    column, core = gy // 2, gy % 2
    first = core == 0
    nz, ny = len(lay.z_parities), len(lay.y_parities)

    swapped = jnp.stack(
        [
            jnp.where(first, receiver_now, source_now),
            jnp.where(first, receiver_prev, source_prev),
            speed_squared,
        ]
    )
    swapped = lax.ppermute(swapped, AXES, lay.core_permutation())
    gathered = gather_traces(lay, traces, receiver_cells)

    grid_y = lay.by * lay.ny
    cell = source_cell[0]
    where = jnp.stack(
        [
            cell // (grid_y * lay.depth) - gx * lay.bx,
            cell // lay.depth % grid_y - column * lay.cy,
            cell % lay.depth,
        ]
    ).astype(jnp.int32)
    amounts = jnp.where(first, wavelet, 0.0)
    times = jnp.where(first, plan[:-1], (steps - 1 - plan[1:])[::-1])

    block = (lay.bx, lay.zt, lay.cy, LANES)
    ext = (lay.ex, lay.zt, lay.ey, LANES)
    field = (lay.bx + 2 * HALO, lay.zt, lay.cy + 2 * HALO, LANES)
    y_rows = lay.zt * ROWS
    z_shape = (lay.bx, lay.zrows, LANES)
    y_shape = (lay.bx, y_rows, LANES)
    d_shape = (REACH, y_rows, LANES)

    outs = [(block, f32)] * 3 + [((lay.bx + 2 * REACH, lay.zrows, LANES), f32)] * nz
    outs += [((3 * lay.bx, y_rows, LANES), f32)] * ny + [(d_shape, f32)] * (nz * ny)
    made = call(
        functools.partial(prepare_kernel, lay),
        outs,
        [source_now, source_prev, receiver_now, receiver_prev, speed_squared, swapped],
    )
    (p, q, s), made = made[:3], made[3:]
    z_out, y_out, d_out = made[:nz], made[nz : nz + ny], made[nz + ny :]
    (planes,) = call(
        functools.partial(planes_kernel, lay),
        [((lay.ex, lay.ey, LANES), f32)],
        [gathered],
        [pltpu.VMEM((lay.ex * lay.ey, LANES), f32)],
    )

    fields = []
    for time in range(0, steps, 2):
        begin, end = time == 0, time + 2 == steps
        z_in = [lax.ppermute(m, AXES, lay.z_permutation(pz)) for m, pz in zip(z_out, lay.z_parities)]
        y_in = [lax.ppermute(m, AXES, lay.y_permutation(py)) for m, py in zip(y_out, lay.y_parities)]
        diagonals = [lay.d_permutation(pz, py) for pz in lay.z_parities for py in lay.y_parities]
        d_in = [lax.ppermute(m, AXES, pairs) for m, pairs in zip(d_out, diagonals)]
        outs, scratch = [(block, f32)] * 2, []
        if end:
            scratch.append(pltpu.VMEM(ext, f32))
        else:
            outs += [(ext, f32), (z_shape, f32)] + [(y_shape, f32)] * ny + [(d_shape, f32)] * (nz * ny)
            if begin:
                outs.append((ext, f32))
                scratch.append(pltpu.VMEM(ext, f32))
        scratch.append(pltpu.VMEM(field, f32))
        made = call(
            functools.partial(round_kernel, lay, time, begin, end),
            outs,
            [amounts, where, p, q, s, planes, *z_in, *y_in, *d_in],
            scratch,
            scalars=2,
        )
        fields += made[:2]
        if not end:
            p, q, z_out = made[1], made[2], [made[3]] * nz
            y_out, d_out = made[4 : 4 + ny], made[4 + ny : 4 + ny + nz * ny]
            if begin:
                s = made[-1]

    kept = (slots + 1, lay.bx, lay.zt, lay.by, LANES)
    own, theirs = call(
        functools.partial(collect_kernel, lay), [(kept, f32)] * 2, [times, *fields], scalars=1
    )
    theirs = lax.ppermute(theirs, AXES, lay.core_permutation())
    shape = source_now.shape
    return tuple(
        call(
            functools.partial(finish_kernel, lay),
            [(shape, f32)] * 4 + [(stored_snapshots.shape, jnp.bfloat16), (shape, f32)],
            [own, theirs, stored_snapshots, image_before],
        )
    )


def solution(mesh):
    block = P(("shot", "gx"), "gy", None)
    line = P("shot", ("gx", "gy"))
    volume = P("shot", "gx", "gy", None)
    return jax.shard_map(
        functools.partial(body, mesh),
        mesh=mesh,
        in_specs=(block,) * 5 + (P("shot"), P("shot"), line, line, P("shot"), volume, block),
        out_specs=(block,) * 4 + (volume, block),
        check_vma=False,
    )
```

```python
import functools

import jax
import jax.numpy as jnp
from jax import lax
from jax.experimental import pallas as pl
from jax.experimental.pallas import tpu as pltpu
from jax.sharding import PartitionSpec as P

STENCIL_COEFFS = (-205.0 / 72.0, 8.0 / 5.0, -1.0 / 5.0, 8.0 / 315.0, -1.0 / 560.0)
REACH = 4
HALO = 2 * REACH
LANES = 128
ROWS = 8
AXES = ("gx", "gy")


class Layout:
    def __init__(self, mesh, block_x, block_y, depth, steps, slots):
        self.nx, self.ny = mesh.shape["gx"], mesh.shape["gy"]
        self.columns = self.ny // 2
        self.bx, self.by, self.depth = block_x, block_y, depth
        self.steps, self.slots = steps, slots
        self.cy = 2 * block_y
        self.zt = pl.cdiv(depth + REACH, LANES)
        self.rest = depth - (self.zt - 1) * LANES
        self.packed = 0 < self.rest <= LANES // 2
        self.ex, self.ey = block_x + 2 * REACH, self.cy + 2 * REACH
        self.zrows = self.cy * (self.zt - 1) + self.cy // 2 if self.packed else self.cy * self.zt
        self.z_parities = [p for p in (0, 1) if p + 1 < self.nx]
        self.y_parities = [p for p in (0, 1) if p + 1 < self.columns]
        assert self.ny % 2 == 0 and block_x >= HALO and block_y % ROWS == 0 and steps % 2 == 0

    def device(self, x, column, core):
        return x * self.ny + 2 * column + core

    def permutation(self, move):
        pairs = []
        for x in range(self.nx):
            for column in range(self.columns):
                other = move(x, column)
                there = 0 <= other[0] < self.nx and 0 <= other[1] < self.columns
                for core in (0, 1):
                    target = self.device(*other, core) if there else self.device(x, column, 1 - core)
                    pairs.append((self.device(x, column, core), target))
        return pairs

    def z_permutation(self, pz):
        return self.permutation(lambda x, c: (x + (1 if x % 2 == pz else -1), c))

    def y_permutation(self, py):
        return self.permutation(lambda x, c: (x, c + (1 if c % 2 == py else -1)))

    def d_permutation(self, pz, py):
        return self.permutation(
            lambda x, c: (x + (1 if x % 2 == pz else -1), c + (1 if c % 2 == py else -1))
        )

    def core_permutation(self):
        return self.permutation(lambda x, c: (-1, -1))

    def place(self):
        gx, gy = lax.axis_index("gx"), lax.axis_index("gy")
        return gx, gy // 2, gy % 2

    def z_side(self, pz):
        gx, _, _ = self.place()
        right = gx % 2 == pz
        return right, jnp.where(right, gx + 1 < self.nx, gx > 0)

    def y_side(self, py):
        _, column, _ = self.place()
        high = column % 2 == py
        return high, jnp.where(high, column + 1 < self.columns, column > 0)


def lane_ids(rows):
    return lax.broadcasted_iota(jnp.int32, (rows, LANES), 1)


def pack(tiles, lay, rows):
    if not lay.packed:
        return list(tiles)
    last = tiles[-1]
    return list(tiles[:-1]) + [last[: rows // 2] + pltpu.roll(last[rows // 2 :], LANES // 2, 1)]


def unpack(block, lay, rows):
    tiles = [block[t * rows : (t + 1) * rows] for t in range(lay.zt - 1)]
    start = (lay.zt - 1) * rows
    if not lay.packed:
        return tiles + [block[start : start + rows]]
    both = block[start : start + rows // 2]
    low = lane_ids(rows // 2) < LANES // 2
    first = jnp.where(low, both, 0.0)
    second = pltpu.roll(jnp.where(low, 0.0, both), LANES // 2, 1)
    return tiles + [jnp.concatenate([first, second], 0)]


def store_packed(ref, index, tiles, lay, rows):
    row = 0
    for piece in pack(tiles, lay, rows):
        ref[index, row : row + piece.shape[0], :] = piece
        row += piece.shape[0]


def write_y_message(ref, lead, source, lay, high):
    for x in range(lay.bx):
        for t in range(lay.zt):
            rows = jnp.where(
                high, source[x, t, lay.cy - ROWS : lay.cy, :], source[x, t, 0:ROWS, :]
            )
            ref[lead * lay.bx + x, t * ROWS : (t + 1) * ROWS, :] = rows


def write_d_message(ref, source, lay, right, high):
    start = jnp.where(right, lay.bx - REACH, 0)
    upper = lax.broadcasted_iota(jnp.int32, (ROWS, LANES), 0) < REACH
    for x in range(REACH // 2):
        for t in range(lay.zt):
            a, b = (
                jnp.where(
                    high,
                    source[start + plane, t, lay.cy - ROWS : lay.cy, :],
                    source[start + plane, t, 0:ROWS, :],
                )
                for plane in (x, x + REACH // 2)
            )
            last = jnp.where(upper, pltpu.roll(a, REACH, 0), b)
            first = jnp.where(upper, a, pltpu.roll(b, REACH, 0))
            ref[x, t * ROWS : (t + 1) * ROWS, :] = jnp.where(high, last, first)


def prepare_kernel(lay, *refs):
    (src_now, src_prev, rec_now, rec_prev, speed, other), refs = refs[:6], refs[6:]
    (p, q, s), refs = refs[:3], refs[3:]
    nz, ny = len(lay.z_parities), len(lay.y_parities)
    z_messages, refs = refs[:nz], refs[nz:]
    y_messages, d_messages = refs[:ny], refs[ny:]
    _, _, core = lay.place()
    first = core == 0
    edge = (lay.zt - 1) * LANES
    for ref in (p, q, s):
        ref[:, lay.zt - 1, :, :] = jnp.zeros((lay.bx, lay.cy, LANES), jnp.float32)
    for index, (ref, a, b) in enumerate(((p, src_now, rec_now), (q, src_prev, rec_prev), (s, speed, speed))):
        for x in range(lay.bx):
            for t in range(lay.zt):
                width = LANES if t + 1 < lay.zt else lay.rest
                lanes = slice(t * LANES, t * LANES + width)
                mine = a[x, :, lanes] if a is b else jnp.where(first, a[x, :, lanes], b[x, :, lanes])
                theirs = other[index, x, :, lanes]
                ref[x, t, 0 : lay.by, 0:width] = jnp.where(first, mine, theirs)
                ref[x, t, lay.by : lay.cy, 0:width] = jnp.where(first, theirs, mine)
    sides = [lay.z_side(pz)[0] for pz in lay.z_parities]
    for x in range(lay.bx):
        tiles = [p[x, t] for t in range(lay.zt)]
        for message in z_messages:
            store_packed(message, x, tiles, lay, lay.cy)
    for message, right in zip(z_messages, sides):
        start = jnp.where(right, lay.bx - REACH, 0)
        for lead, ref in ((0, q), (1, s)):
            for x in range(REACH):
                tiles = [ref[start + x, t] for t in range(lay.zt)]
                store_packed(message, lay.bx + lead * REACH + x, tiles, lay, lay.cy)
    highs = [lay.y_side(py)[0] for py in lay.y_parities]
    for message, high in zip(y_messages, highs):
        for lead, ref in enumerate((p, q, s)):
            write_y_message(message, lead, ref, lay, high)
    corners = [(right, high) for right in sides for high in highs]
    for message, (right, high) in zip(d_messages, corners):
        write_d_message(message, p, lay, right, high)


def planes_kernel(lay, gathered, planes, total):
    gx, column, core = lay.place()
    start_x, start_y = gx * lay.bx - REACH, column * lay.cy - REACH
    cells = lay.ex * lay.ey
    padded = gathered.shape[1]
    total[...] = jnp.zeros_like(total)

    def add(index, carry):
        values = gathered[index]
        x = values[lay.steps : lay.steps + 1, :].astype(jnp.int32) - start_x
        y = values[lay.steps + 1 : lay.steps + 2, :].astype(jnp.int32) - start_y
        inside = (x >= 0) & (x < lay.ex) & (y >= 0) & (y < lay.ey)
        cell = jnp.where(inside, x * lay.ey + y, -1)
        ids = lax.broadcasted_iota(jnp.int32, (cells, LANES), 0)
        chosen = jnp.where(ids == cell, 1.0, 0.0).astype(jnp.bfloat16)
        high = values.astype(jnp.bfloat16)
        rest = values - high.astype(jnp.float32)
        middle = rest.astype(jnp.bfloat16)
        low = (rest - middle.astype(jnp.float32)).astype(jnp.bfloat16)
        fill = jnp.zeros((LANES - 3 * padded, LANES), jnp.bfloat16)
        parts = jnp.concatenate([high, middle, low, fill], 0)
        total[...] += lax.dot_general(
            chosen, parts, (((1,), (1,)), ((), ())), preferred_element_type=jnp.float32
        )
        return carry

    lax.fori_loop(0, gathered.shape[0], add, 0)
    summed = total[...]
    summed = (
        summed + pltpu.roll(summed, LANES - padded, 1) + pltpu.roll(summed, LANES - 2 * padded, 1)
    )
    summed = jnp.where(core == 1, summed, 0.0)
    planes[...] = summed.reshape(lay.ex, lay.ey, LANES)


def advance(lay, field, x, y, rows, before, speed, injected):
    lane = lane_ids(rows)
    centre = [field[x, t, y : y + rows, :] for t in range(lay.zt)]
    sums = []
    for k in range(1, REACH + 1):
        left = [pltpu.roll(c, k, 1) for c in centre]
        right = [pltpu.roll(c, LANES - k, 1) for c in centre]
        per_tile = []
        for t in range(lay.zt):
            lower = jnp.where(lane < k, left[t - 1], left[t])
            upper = jnp.where(lane < LANES - k, right[t], right[(t + 1) % lay.zt])
            around = field[x - k, t, y : y + rows, :] + field[x + k, t, y : y + rows, :]
            around += field[x, t, y - k : y - k + rows, :] + field[x, t, y + k : y + k + rows, :]
            per_tile.append(around + (lower + upper))
        sums.append(per_tile)
    out = []
    for t in range(lay.zt):
        drive = 3.0 * STENCIL_COEFFS[0] * centre[t]
        for k in range(REACH):
            drive += STENCIL_COEFFS[k + 1] * sums[k][t]
        if t == 0:
            drive += injected
        out.append(2.0 * centre[t] - before[t] + speed[t] * drive)
    return out


def round_kernel(lay, time, first, last, *refs):
    nz, ny = len(lay.z_parities), len(lay.y_parities)
    (wavelet, where, p, q, s, planes), refs = refs[:6], refs[6:]
    z_in, refs = refs[:nz], refs[nz:]
    y_in, refs = refs[:ny], refs[ny:]
    d_in, refs = refs[: nz * ny], refs[nz * ny :]
    (middle, latest), refs = refs[:2], refs[2:]
    if last:
        q_out, buffer = refs[:2]
    else:
        (q_out, z_out), refs = refs[:2], refs[2:]
        y_out, refs = refs[:ny], refs[ny:]
        d_out, refs = refs[: nz * ny], refs[nz * ny :]
        if first:
            s_out, q_ext, buffer = refs
        else:
            (buffer,) = refs
    z_sides = [lay.z_side(pz) for pz in lay.z_parities]
    y_sides = [lay.y_side(py) for py in lay.y_parities]
    bx, cy, zt = lay.bx, lay.cy, lay.zt
    own_x, own_y = HALO, HALO

    buffer[own_x : own_x + bx, :, own_y : own_y + cy, :] = p[...]
    if nz < 2:
        buffer[0:own_x] = jnp.zeros((own_x,) + buffer.shape[1:], jnp.float32)
        buffer[own_x + bx :] = jnp.zeros((own_x,) + buffer.shape[1:], jnp.float32)
    if ny < 2:
        empty = (bx + 2 * REACH, zt, HALO, LANES)
        buffer[own_x - REACH : own_x + bx + REACH, :, 0:own_y, :] = jnp.zeros(empty, jnp.float32)
        buffer[own_x - REACH : own_x + bx + REACH, :, own_y + cy :, :] = jnp.zeros(empty, jnp.float32)
    for (right, valid), message in zip(z_sides, z_in):
        start = jnp.where(right, own_x + bx, 0)
        skip = jnp.where(right, 0, bx - HALO)
        for x in range(HALO):
            block = jnp.where(valid, message[skip + x], 0.0)
            for t, tile in enumerate(unpack(block, lay, cy)):
                buffer[start + x, t, own_y : own_y + cy, :] = tile
    for (high, valid), message in zip(y_sides, y_in):
        start = pl.multiple_of(jnp.where(high, own_y + cy, own_y - ROWS), ROWS)
        for x in range(bx):
            for t in range(zt):
                rows = message[x, t * ROWS : (t + 1) * ROWS, :]
                buffer[own_x + x, t, pl.ds(start, ROWS), :] = jnp.where(valid, rows, 0.0)
    corners = [(r, h, u & v) for r, u in z_sides for h, v in y_sides]
    for (right, high, valid), message in zip(corners, d_in):
        x_start = jnp.where(right, own_x + bx, own_x - REACH)
        start = pl.multiple_of(jnp.where(high, own_y + cy, own_y - ROWS), ROWS)
        for x in range(REACH // 2):
            for t in range(zt):
                rows = jnp.where(valid, message[x, t * ROWS : (t + 1) * ROWS, :], 0.0)
                turned = pltpu.roll(rows, REACH, 0)
                buffer[x_start + x, t, pl.ds(start, ROWS), :] = jnp.where(high, rows, turned)
                buffer[x_start + x + REACH // 2, t, pl.ds(start, ROWS), :] = jnp.where(high, turned, rows)

    if first:
        for lead, own, ext in ((0, q, q_ext), (1, s, s_out)):
            ext[...] = jnp.zeros_like(ext)
            for x in range(bx):
                for t in range(zt):
                    ext[REACH + x, t, REACH : REACH + cy, :] = own[x, t]
            for (right, valid), message in zip(z_sides, z_in):
                start = jnp.where(right, REACH + bx, 0)
                for x in range(REACH):
                    block = jnp.where(valid, message[bx + lead * REACH + x], 0.0)
                    for t, tile in enumerate(unpack(block, lay, cy)):
                        ext[start + x, t, REACH : REACH + cy, :] = tile
            for is_high, start, cut in ((False, 0, ROWS - REACH), (True, REACH + cy, 0)):
                wants = [v & (h if is_high else ~h) for h, v in y_sides]
                for x in range(bx):
                    for t in range(zt):
                        rows = slice(t * ROWS + cut, t * ROWS + cut + REACH)
                        ext[REACH + x, t, start : start + REACH, :] = sum(
                            (jnp.where(w, m[(lead + 1) * bx + x, rows, :], 0.0) for w, m in zip(wants, y_in)),
                            jnp.zeros((REACH, LANES), jnp.float32),
                        )
        q, s = q_ext, s_out

    def injected(x, rows, y, back):
        values = pltpu.roll(planes[x], LANES - back, 1) if back else planes[x]
        return jnp.where(lane_ids(lay.ey) == 0, values, 0.0)[y : y + rows]

    def add_source(target, speed_rows, x, y, count_x, count_y, amount):
        @pl.when((x >= 0) & (x < count_x) & (y >= 0) & (y < count_y))
        def _():
            depth = where[2]
            tile, lane = depth // LANES, depth % LANES
            shape = (count_y, LANES)
            here = (lax.broadcasted_iota(jnp.int32, shape, 0) == y) & (
                lax.broadcasted_iota(jnp.int32, shape, 1) == lane
            )
            target[x, tile] += jnp.where(here, speed_rows(x, tile) * amount, 0.0)

    for x in range(lay.ex):
        inside = REACH <= x < REACH + bx
        y, count = (0, lay.ey) if inside else (REACH, cy)
        out = advance(
            lay, buffer, x + REACH, y + REACH, count,
            [q[x, t, y : y + count, :] for t in range(zt)],
            [s[x, t, y : y + count, :] for t in range(zt)],
            injected(x, count, y, lay.steps - 1 - time),
        )
        for t in range(zt):
            q_out[x, t, y : y + count, :] = out[t]
    add_source(q_out, lambda x, t: s[x, t], where[0] + REACH, where[1] + REACH, lay.ex, lay.ey, wavelet[time])

    for x in range(bx):
        out = advance(
            lay, q_out, x + REACH, REACH, cy,
            [p[x, t] for t in range(zt)],
            [s[x + REACH, t, REACH : REACH + cy, :] for t in range(zt)],
            injected(x + REACH, cy, REACH, lay.steps - 2 - time),
        )
        for t in range(zt):
            latest[x, t] = out[t]
            middle[x, t] = q_out[x + REACH, t, REACH : REACH + cy, :]
    add_source(
        latest, lambda x, t: s[x + REACH, t, REACH : REACH + cy, :], where[0], where[1], bx, cy, wavelet[time + 1]
    )

    if not last:
        for x in range(bx):
            store_packed(z_out, x, [latest[x, t] for t in range(zt)], lay, cy)
        for message, (high, _) in zip(y_out, y_sides):
            write_y_message(message, 0, latest, lay, high)
        corners = [(right, high) for right, _ in z_sides for high, _ in y_sides]
        for message, (right, high) in zip(d_out, corners):
            write_d_message(message, latest, lay, right, high)


def collect_kernel(lay, times, *refs):
    fields, own, theirs = refs[: lay.steps], refs[lay.steps], refs[lay.steps + 1]
    _, _, core = lay.place()

    def put(index, field):
        for x in range(lay.bx):
            for t in range(lay.zt):
                low, high = field[x, t, 0 : lay.by, :], field[x, t, lay.by : lay.cy, :]
                own[index, x, t] = jnp.where(core == 0, low, high)
                theirs[index, x, t] = jnp.where(core == 0, high, low)

    put(0, fields[lay.steps - 2])
    put(1, fields[lay.steps - 1])
    for slot in range(lay.slots - 1):
        for time in range(lay.steps):
            pl.when(times[slot] == time)(functools.partial(put, 2 + slot, fields[time]))


def finish_kernel(lay, own, theirs, stored, image_before, *outs):
    src_prev, src_now, rec_prev, rec_now, snapshots, image = outs
    _, _, core = lay.place()
    first = core == 0
    for x in range(lay.bx):
        for t in range(lay.zt):
            width = LANES if t + 1 < lay.zt else lay.rest
            lanes = slice(t * LANES, t * LANES + width)
            source = [jnp.where(first, own[i, x, t], theirs[i, x, t])[:, :width] for i in range(lay.slots + 1)]
            receiver = [jnp.where(first, theirs[i, x, t], own[i, x, t])[:, :width] for i in range(lay.slots + 1)]
            src_prev[x, :, lanes], src_now[x, :, lanes] = source[0], source[1]
            rec_prev[x, :, lanes], rec_now[x, :, lanes] = receiver[0], receiver[1]
            total = image_before[x, :, lanes]
            for slot in range(lay.slots):
                kept = source[1] if slot == lay.slots - 1 else source[2 + slot]
                snapshots[slot, x, :, lanes] = kept.astype(jnp.bfloat16)
                crossed = receiver[1] if slot == 0 else receiver[1 + lay.slots - slot]
                total += stored[slot, x, :, lanes].astype(jnp.float32) * crossed
            image[x, :, lanes] = total


def call(kernel, outs, operands, scratch=(), scalars=0):
    in_specs = [pl.BlockSpec(memory_space=pltpu.SMEM)] * scalars
    in_specs += [pl.BlockSpec(memory_space=pltpu.VMEM)] * (len(operands) - scalars)
    return pl.pallas_call(
        kernel,
        out_shape=[jax.ShapeDtypeStruct(shape, dtype) for shape, dtype in outs],
        in_specs=in_specs,
        out_specs=[pl.BlockSpec(memory_space=pltpu.VMEM)] * len(outs),
        scratch_shapes=list(scratch),
        compiler_params=pltpu.CompilerParams(vmem_limit_bytes=16 * 1024 * 1024),
    )(*operands)


def gather_traces(lay, traces, receiver_cells):
    grid_y = lay.by * lay.ny
    cells = receiver_cells
    rows = [traces, (cells // grid_y).astype(jnp.float32), (cells % grid_y).astype(jnp.float32)]
    padded = pl.cdiv(lay.steps + 2, 2 * ROWS) * 2 * ROWS
    rows.append(jnp.zeros((padded - lay.steps - 2, traces.shape[1]), jnp.float32))
    message = jnp.concatenate(rows, 0)
    other = lax.ppermute(message, AXES, lay.core_permutation())
    message = jnp.concatenate([message, other], 1)[None]
    if message.shape[2] != LANES:
        spare = -message.shape[2] % LANES
        fill = jnp.full((1, padded, spare), -1e6, jnp.float32)
        message = jnp.concatenate([message, fill], 2)
        message = message.reshape(padded, -1, LANES).transpose(1, 0, 2)
    for count, move in (
        (lay.columns, lambda x, c, bit: (x, c ^ bit)),
        (lay.nx, lambda x, c, bit: (x ^ bit, c)),
    ):
        assert count & (count - 1) == 0
        bit = 1
        while bit < count:
            pairs = lay.permutation(functools.partial(move, bit=bit))
            message = jnp.concatenate([message, lax.ppermute(message, AXES, pairs)], 0)
            bit *= 2
    return message


def body(
    mesh,
    source_prev,
    source_now,
    receiver_prev,
    receiver_now,
    speed_squared,
    wavelet,
    source_cell,
    traces,
    receiver_cells,
    plan,
    stored_snapshots,
    image_before,
):
    steps, slots = wavelet.shape[0], plan.shape[0]
    lay = Layout(mesh, *source_now.shape, steps, slots)
    f32 = jnp.float32
    gx, gy = lax.axis_index("gx"), lax.axis_index("gy")
    column, core = gy // 2, gy % 2
    first = core == 0
    nz, ny = len(lay.z_parities), len(lay.y_parities)

    swapped = jnp.stack(
        [
            jnp.where(first, receiver_now, source_now),
            jnp.where(first, receiver_prev, source_prev),
            speed_squared,
        ]
    )
    swapped = lax.ppermute(swapped, AXES, lay.core_permutation())
    gathered = gather_traces(lay, traces, receiver_cells)

    grid_y = lay.by * lay.ny
    cell = source_cell[0]
    where = jnp.stack(
        [
            cell // (grid_y * lay.depth) - gx * lay.bx,
            cell // lay.depth % grid_y - column * lay.cy,
            cell % lay.depth,
        ]
    ).astype(jnp.int32)
    amounts = jnp.where(first, wavelet, 0.0)
    times = jnp.where(first, plan[:-1], (steps - 1 - plan[1:])[::-1])

    block = (lay.bx, lay.zt, lay.cy, LANES)
    ext = (lay.ex, lay.zt, lay.ey, LANES)
    field = (lay.bx + 2 * HALO, lay.zt, lay.cy + 2 * HALO, LANES)
    y_rows = lay.zt * ROWS
    z_shape = (lay.bx, lay.zrows, LANES)
    y_shape = (lay.bx, y_rows, LANES)
    d_shape = (REACH // 2, y_rows, LANES)

    outs = [(block, f32)] * 3 + [((lay.bx + 2 * REACH, lay.zrows, LANES), f32)] * nz
    outs += [((3 * lay.bx, y_rows, LANES), f32)] * ny + [(d_shape, f32)] * (nz * ny)
    made = call(
        functools.partial(prepare_kernel, lay),
        outs,
        [source_now, source_prev, receiver_now, receiver_prev, speed_squared, swapped],
    )
    (p, q, s), made = made[:3], made[3:]
    z_out, y_out, d_out = made[:nz], made[nz : nz + ny], made[nz + ny :]
    (planes,) = call(
        functools.partial(planes_kernel, lay),
        [((lay.ex, lay.ey, LANES), f32)],
        [gathered],
        [pltpu.VMEM((lay.ex * lay.ey, LANES), f32)],
    )

    fields = []
    for time in range(0, steps, 2):
        begin, end = time == 0, time + 2 == steps
        z_in = [lax.ppermute(m, AXES, lay.z_permutation(pz)) for m, pz in zip(z_out, lay.z_parities)]
        y_in = [lax.ppermute(m, AXES, lay.y_permutation(py)) for m, py in zip(y_out, lay.y_parities)]
        diagonals = [lay.d_permutation(pz, py) for pz in lay.z_parities for py in lay.y_parities]
        d_in = [lax.ppermute(m, AXES, pairs) for m, pairs in zip(d_out, diagonals)]
        outs, scratch = [(block, f32)] * 2, []
        if end:
            scratch.append(pltpu.VMEM(ext, f32))
        else:
            outs += [(ext, f32), (z_shape, f32)] + [(y_shape, f32)] * ny + [(d_shape, f32)] * (nz * ny)
            if begin:
                outs.append((ext, f32))
                scratch.append(pltpu.VMEM(ext, f32))
        scratch.append(pltpu.VMEM(field, f32))
        made = call(
            functools.partial(round_kernel, lay, time, begin, end),
            outs,
            [amounts, where, p, q, s, planes, *z_in, *y_in, *d_in],
            scratch,
            scalars=2,
        )
        fields += made[:2]
        if not end:
            p, q, z_out = made[1], made[2], [made[3]] * nz
            y_out, d_out = made[4 : 4 + ny], made[4 + ny : 4 + ny + nz * ny]
            if begin:
                s = made[-1]

    kept = (slots + 1, lay.bx, lay.zt, lay.by, LANES)
    own, theirs = call(
        functools.partial(collect_kernel, lay), [(kept, f32)] * 2, [times, *fields], scalars=1
    )
    theirs = lax.ppermute(theirs, AXES, lay.core_permutation())
    shape = source_now.shape
    return tuple(
        call(
            functools.partial(finish_kernel, lay),
            [(shape, f32)] * 4 + [(stored_snapshots.shape, jnp.bfloat16), (shape, f32)],
            [own, theirs, stored_snapshots, image_before],
        )
    )


def solution(mesh):
    block = P(("shot", "gx"), "gy", None)
    line = P("shot", ("gx", "gy"))
    volume = P("shot", "gx", "gy", None)
    return jax.shard_map(
        functools.partial(body, mesh),
        mesh=mesh,
        in_specs=(block,) * 5 + (P("shot"), P("shot"), line, line, P("shot"), volume, block),
        out_specs=(block,) * 4 + (volume, block),
        check_vma=False,
    )
```

```python
import functools

import jax
import jax.numpy as jnp
from jax import lax
from jax.experimental import pallas as pl
from jax.experimental.pallas import tpu as pltpu
from jax.sharding import PartitionSpec as P

STENCIL_COEFFS = (-205.0 / 72.0, 8.0 / 5.0, -1.0 / 5.0, 8.0 / 315.0, -1.0 / 560.0)
REACH = 4
HALO = 2 * REACH
LANES = 128
ROWS = 8
AXES = ("gx", "gy")


class Layout:
    def __init__(self, mesh, block_x, block_y, depth, steps, slots):
        self.nx, self.ny = mesh.shape["gx"], mesh.shape["gy"]
        self.columns = self.ny // 2
        self.bx, self.by, self.depth = block_x, block_y, depth
        self.steps, self.slots = steps, slots
        self.cy = 2 * block_y
        self.zt = pl.cdiv(depth + REACH, LANES)
        self.rest = depth - (self.zt - 1) * LANES
        self.packed = 0 < self.rest <= LANES // 2
        self.ex, self.ey = block_x + 2 * REACH, self.cy + 2 * REACH
        self.zrows = self.cy * (self.zt - 1) + self.cy // 2 if self.packed else self.cy * self.zt
        self.trace_rows = pl.cdiv(steps + 2, 2 * ROWS) * 2 * ROWS
        self.z_parities = [p for p in (0, 1) if p + 1 < self.nx]
        self.y_parities = [p for p in (0, 1) if p + 1 < self.columns]
        assert self.ny % 2 == 0 and block_x >= HALO and block_y % ROWS == 0 and steps % 2 == 0

    def device(self, x, column, core):
        return x * self.ny + 2 * column + core

    def permutation(self, move):
        pairs = []
        for x in range(self.nx):
            for column in range(self.columns):
                other = move(x, column)
                there = 0 <= other[0] < self.nx and 0 <= other[1] < self.columns
                for core in (0, 1):
                    target = self.device(*other, core) if there else self.device(x, column, 1 - core)
                    pairs.append((self.device(x, column, core), target))
        return pairs

    def z_permutation(self, pz):
        return self.permutation(lambda x, c: (x + (1 if x % 2 == pz else -1), c))

    def y_permutation(self, py):
        return self.permutation(lambda x, c: (x, c + (1 if c % 2 == py else -1)))

    def d_permutation(self, pz, py):
        return self.permutation(
            lambda x, c: (x + (1 if x % 2 == pz else -1), c + (1 if c % 2 == py else -1))
        )

    def carriers(self, z_messages, y_messages, d_messages):
        starts = (self.bx + 2 * REACH, 3 * self.bx, REACH // 2)
        return [(m, start) for ms, start in zip((z_messages, y_messages, d_messages), starts) for m in ms]

    def by_kind(self, messages):
        z, y = bool(self.z_parities), bool(self.y_parities)
        return messages[:z], messages[z : z + y], messages[z + y :]

    def spot(self, message, start, group, part):
        chunk = group * (self.trace_rows // ROWS) + part
        per_plane = message.shape[1] // ROWS
        row = chunk % per_plane * ROWS
        return start + chunk // per_plane, row if isinstance(row, int) else pl.multiple_of(row, ROWS)

    def core_permutation(self):
        return self.permutation(lambda x, c: (-1, -1))

    def place(self):
        gx, gy = lax.axis_index("gx"), lax.axis_index("gy")
        return gx, gy // 2, gy % 2

    def z_side(self, pz):
        gx, _, _ = self.place()
        right = gx % 2 == pz
        return right, jnp.where(right, gx + 1 < self.nx, gx > 0)

    def y_side(self, py):
        _, column, _ = self.place()
        high = column % 2 == py
        return high, jnp.where(high, column + 1 < self.columns, column > 0)


def lane_ids(rows):
    return lax.broadcasted_iota(jnp.int32, (rows, LANES), 1)


def pack(tiles, lay, rows):
    if not lay.packed:
        return list(tiles)
    last = tiles[-1]
    return list(tiles[:-1]) + [last[: rows // 2] + pltpu.roll(last[rows // 2 :], LANES // 2, 1)]


def unpack(block, lay, rows):
    tiles = [block[t * rows : (t + 1) * rows] for t in range(lay.zt - 1)]
    start = (lay.zt - 1) * rows
    if not lay.packed:
        return tiles + [block[start : start + rows]]
    both = block[start : start + rows // 2]
    low = lane_ids(rows // 2) < LANES // 2
    first = jnp.where(low, both, 0.0)
    second = pltpu.roll(jnp.where(low, 0.0, both), LANES // 2, 1)
    return tiles + [jnp.concatenate([first, second], 0)]


def store_packed(ref, index, tiles, lay, rows):
    row = 0
    for piece in pack(tiles, lay, rows):
        ref[index, row : row + piece.shape[0], :] = piece
        row += piece.shape[0]


def write_y_message(ref, lead, source, lay, high):
    for x in range(lay.bx):
        for t in range(lay.zt):
            rows = jnp.where(
                high, source[x, t, lay.cy - ROWS : lay.cy, :], source[x, t, 0:ROWS, :]
            )
            ref[lead * lay.bx + x, t * ROWS : (t + 1) * ROWS, :] = rows


def write_d_message(ref, source, lay, right, high):
    start = jnp.where(right, lay.bx - REACH, 0)
    upper = lax.broadcasted_iota(jnp.int32, (ROWS, LANES), 0) < REACH
    for x in range(REACH // 2):
        for t in range(lay.zt):
            a, b = (
                jnp.where(
                    high,
                    source[start + plane, t, lay.cy - ROWS : lay.cy, :],
                    source[start + plane, t, 0:ROWS, :],
                )
                for plane in (x, x + REACH // 2)
            )
            last = jnp.where(upper, pltpu.roll(a, REACH, 0), b)
            first = jnp.where(upper, a, pltpu.roll(b, REACH, 0))
            ref[x, t * ROWS : (t + 1) * ROWS, :] = jnp.where(high, last, first)


def load_kernel(lay, src_now, src_prev, rec_now, rec_prev, speed, traces, cells, mine, swap, message, *scratch):
    held, samples, numbers, semaphores = scratch
    copies = [
        (src_now, held.at[0]),
        (rec_now, held.at[1]),
        (src_prev, held.at[2]),
        (rec_prev, held.at[3]),
        (speed, mine.at[2]),
        (speed, swap.at[2]),
        (traces, samples),
        (cells, numbers),
    ]
    copies = [pltpu.make_async_copy(a, b, semaphores.at[i]) for i, (a, b) in enumerate(copies)]
    for copy in copies:
        copy.start()
    for copy in copies:
        copy.wait()
    _, _, core = lay.place()
    for index in range(2):
        for x in range(lay.bx):
            source, receiver = held[2 * index, x], held[2 * index + 1, x]
            mine[index, x] = jnp.where(core == 0, source, receiver)
            swap[index, x] = jnp.where(core == 0, receiver, source)
    cell = numbers[...].astype(jnp.float32)
    row = jnp.floor((cell + 0.5) * (1.0 / (lay.by * lay.ny)))
    message[...] = jnp.zeros_like(message)
    message[0 : lay.steps, :] = samples[...]
    message[lay.steps : lay.steps + 1, :] = row
    message[lay.steps + 1 : lay.steps + 2, :] = cell - row * (lay.by * lay.ny)


def prepare_kernel(lay, *refs):
    (own, other), refs = refs[:2], refs[2:]
    (p, q, s), refs = refs[:3], refs[3:]
    nz, ny = len(lay.z_parities), len(lay.y_parities)
    z_messages, refs = refs[:nz], refs[nz:]
    y_messages, d_messages = refs[:ny], refs[ny:]
    _, _, core = lay.place()
    first = core == 0
    edge = (lay.zt - 1) * LANES
    for ref in (p, q, s):
        ref[:, lay.zt - 1, :, :] = jnp.zeros((lay.bx, lay.cy, LANES), jnp.float32)
    for index, ref in enumerate((p, q, s)):
        for x in range(lay.bx):
            for t in range(lay.zt):
                width = LANES if t + 1 < lay.zt else lay.rest
                lanes = slice(t * LANES, t * LANES + width)
                mine = own[index, x, :, lanes]
                theirs = other[index, x, :, lanes]
                ref[x, t, 0 : lay.by, 0:width] = jnp.where(first, mine, theirs)
                ref[x, t, lay.by : lay.cy, 0:width] = jnp.where(first, theirs, mine)
    sides = [lay.z_side(pz)[0] for pz in lay.z_parities]
    for x in range(lay.bx):
        tiles = [p[x, t] for t in range(lay.zt)]
        for message in z_messages:
            store_packed(message, x, tiles, lay, lay.cy)
    for message, right in zip(z_messages, sides):
        start = jnp.where(right, lay.bx - REACH, 0)
        for lead, ref in ((0, q), (1, s)):
            for x in range(REACH):
                tiles = [ref[start + x, t] for t in range(lay.zt)]
                store_packed(message, lay.bx + lead * REACH + x, tiles, lay, lay.cy)
    highs = [lay.y_side(py)[0] for py in lay.y_parities]
    for message, high in zip(y_messages, highs):
        for lead, ref in enumerate((p, q, s)):
            write_y_message(message, lead, ref, lay, high)
    corners = [(right, high) for right in sides for high in highs]
    for message, (right, high) in zip(d_messages, corners):
        write_d_message(message, p, lay, right, high)


def append_kernel(lay, *refs):
    groups, messages = refs[0], refs[1 + (len(refs) - 1) // 2 :]
    for message, start in lay.carriers(*lay.by_kind(messages)):
        for group in range(groups.shape[0]):
            for part in range(lay.trace_rows // ROWS):
                plane, row = lay.spot(message, start, group, part)
                message[plane, row : row + ROWS, :] = groups[group, part * ROWS : (part + 1) * ROWS, :]


def planes_kernel(lay, *refs):
    groups, messages, (planes, total) = refs[0], refs[1:-2], refs[-2:]
    carriers = lay.carriers(*lay.by_kind(messages))
    gx, column, core = lay.place()
    start_x, start_y = gx * lay.bx - REACH, column * lay.cy - REACH
    cells = lay.ex * lay.ey
    padded = lay.trace_rows
    total[...] = jnp.zeros_like(total)

    def add(values):
        x = values[lay.steps : lay.steps + 1, :].astype(jnp.int32) - start_x
        y = values[lay.steps + 1 : lay.steps + 2, :].astype(jnp.int32) - start_y
        inside = (x >= 0) & (x < lay.ex) & (y >= 0) & (y < lay.ey)
        cell = jnp.where(inside, x * lay.ey + y, -1)
        ids = lax.broadcasted_iota(jnp.int32, (cells, LANES), 0)
        chosen = jnp.where(ids == cell, 1.0, 0.0).astype(jnp.bfloat16)
        high = values.astype(jnp.bfloat16)
        rest = values - high.astype(jnp.float32)
        middle = rest.astype(jnp.bfloat16)
        low = (rest - middle.astype(jnp.float32)).astype(jnp.bfloat16)
        fill = jnp.zeros((LANES - 3 * padded, LANES), jnp.bfloat16)
        parts = jnp.concatenate([high, middle, low, fill], 0)
        total[...] += lax.dot_general(
            chosen, parts, (((1,), (1,)), ((), ())), preferred_element_type=jnp.float32
        )

    def add_groups(group, carry):
        add(groups[group])
        for message, start in carriers:
            parts = []
            for part in range(padded // ROWS):
                plane, row = lay.spot(message, start, group, part)
                parts.append(message[plane, pl.ds(row, ROWS), :])
            add(jnp.concatenate(parts, 0))
        return carry

    lax.fori_loop(0, groups.shape[0], add_groups, 0, unroll=groups.shape[0] <= 2)
    summed = total[...]
    summed = (
        summed + pltpu.roll(summed, LANES - padded, 1) + pltpu.roll(summed, LANES - 2 * padded, 1)
    )
    summed = jnp.where(core == 1, summed, 0.0)
    planes[...] = summed.reshape(lay.ex, lay.ey, LANES)


def advance(lay, field, x, y, rows, before, speed):
    lane = lane_ids(rows)
    centre = [field[x, t, y : y + rows, :] for t in range(lay.zt)]
    sums = []
    for k in range(1, REACH + 1):
        left = [pltpu.roll(c, k, 1) for c in centre]
        right = [pltpu.roll(c, LANES - k, 1) for c in centre]
        per_tile = []
        for t in range(lay.zt):
            lower = jnp.where(lane < k, left[t - 1], left[t])
            upper = jnp.where(lane < LANES - k, right[t], right[(t + 1) % lay.zt])
            around = field[x - k, t, y : y + rows, :] + field[x + k, t, y : y + rows, :]
            around += field[x, t, y - k : y - k + rows, :] + field[x, t, y + k : y + k + rows, :]
            per_tile.append(around + (lower + upper))
        sums.append(per_tile)
    out = []
    for t in range(lay.zt):
        drive = 3.0 * STENCIL_COEFFS[0] * centre[t]
        for k in range(REACH):
            drive += STENCIL_COEFFS[k + 1] * sums[k][t]
        out.append(2.0 * centre[t] - before[t] + speed[t] * drive)
    return out


def side_kernel(lay, time, *refs):
    nz, ny = len(lay.z_parities), len(lay.y_parities)
    (p, q, s), refs = refs[:3], refs[3:]
    first = time == 0
    if not first:
        p = p.at[time - 1]
    z_in, refs = refs[:nz], refs[nz:]
    y_in, refs = refs[:ny], refs[ny:]
    stepped, buffer = refs[0], refs[-1]
    z_sides = [lay.z_side(pz) for pz in lay.z_parities]
    y_sides = [lay.y_side(py) for py in lay.y_parities]
    bx, cy, zt = lay.bx, lay.cy, lay.zt
    own_x, own_y = HALO, HALO

    buffer[own_x : own_x + bx, :, own_y : own_y + cy, :] = p[...]
    around = ((own_x - REACH, own_x), (own_x + bx, own_x + bx + REACH))
    for low, high in around if ny == 2 else ((own_x - REACH, own_x + bx + REACH),):
        empty = jnp.zeros((high - low, zt, HALO, LANES), jnp.float32)
        buffer[low:high, :, 0:own_y, :] = empty
        buffer[low:high, :, own_y + cy :, :] = empty
    if nz < 2:
        empty = jnp.zeros((own_x, zt, cy, LANES), jnp.float32)
        buffer[0:own_x, :, own_y : own_y + cy, :] = empty
        buffer[own_x + bx :, :, own_y : own_y + cy, :] = empty
    for (right, valid), message in zip(z_sides, z_in):
        start = jnp.where(right, own_x + bx, 0)
        skip = jnp.where(right, 0, bx - HALO)
        for x in range(HALO):
            block = jnp.where(valid, message[skip + x], 0.0)
            for t, tile in enumerate(unpack(block, lay, cy)):
                buffer[start + x, t, own_y : own_y + cy, :] = tile
    for (high, valid), message in zip(y_sides, y_in):
        start = pl.multiple_of(jnp.where(high, own_y + cy, own_y - ROWS), ROWS)
        for x in range(bx):
            for t in range(zt):
                rows = message[x, t * ROWS : (t + 1) * ROWS, :]
                buffer[own_x + x, t, pl.ds(start, ROWS), :] = jnp.where(valid, rows, 0.0)

    if first:
        s_out, q_ext = refs[1:3]
        for lead, own, ext in ((0, q, q_ext), (1, s, s_out)):
            ext[...] = jnp.zeros_like(ext)
            for x in range(bx):
                for t in range(zt):
                    ext[REACH + x, t, REACH : REACH + cy, :] = own[x, t]
            for (right, valid), message in zip(z_sides, z_in):
                start = jnp.where(right, REACH + bx, 0)
                for x in range(REACH):
                    block = jnp.where(valid, message[bx + lead * REACH + x], 0.0)
                    for t, tile in enumerate(unpack(block, lay, cy)):
                        ext[start + x, t, REACH : REACH + cy, :] = tile
            for is_high, start, cut in ((False, 0, ROWS - REACH), (True, REACH + cy, 0)):
                wants = [v & (h if is_high else ~h) for h, v in y_sides]
                for x in range(bx):
                    for t in range(zt):
                        rows = slice(t * ROWS + cut, t * ROWS + cut + REACH)
                        ext[REACH + x, t, start : start + REACH, :] = sum(
                            (jnp.where(w, m[(lead + 1) * bx + x, rows, :], 0.0) for w, m in zip(wants, y_in)),
                            jnp.zeros((REACH, LANES), jnp.float32),
                        )
        q, s = q_ext, s_out

    for x in range(lay.ex):
        inside = REACH <= x < REACH + bx
        y, count = (0, lay.ey) if inside else (REACH, cy)
        out = advance(
            lay, buffer, x + REACH, y + REACH, count,
            [q[x, t, y : y + count, :] for t in range(zt)],
            [s[x, t, y : y + count, :] for t in range(zt)],
        )
        for t in range(zt):
            stepped[x, t, y : y + count, :] = out[t]


def add_corner(lay, field, s, message, right, high, valid, corner):
    empty = jnp.zeros((REACH, lay.zt, ROWS, LANES), jnp.float32)
    corner[:, :, 0:ROWS, :] = empty
    corner[:, :, 2 * ROWS :, :] = empty
    upper = lax.broadcasted_iota(jnp.int32, (ROWS, LANES), 0) < REACH
    near = jnp.where(upper, 1.0, 0.0)
    keep = jnp.where(valid, jnp.where(high, near, 1.0 - near), 0.0)
    for x in range(REACH // 2):
        for t in range(lay.zt):
            rows = message[x, t * ROWS : (t + 1) * ROWS, :]
            turned = pltpu.roll(rows, REACH, 0)
            corner[x, t, ROWS : 2 * ROWS, :] = jnp.where(high, rows, turned) * keep
            corner[x + REACH // 2, t, ROWS : 2 * ROWS, :] = jnp.where(high, turned, rows) * keep
    high_share, low_share = jnp.where(high, 1.0, 0.0), jnp.where(high, 0.0, 1.0)
    planes_start = jnp.where(right, REACH + lay.bx, 0)
    rows_start = jnp.where(right, lay.bx, REACH)
    for x in range(REACH):
        for t in range(lay.zt):
            above = sum(STENCIL_COEFFS[k] * corner[x, t, k : k + ROWS, :] for k in range(1, REACH + 1))
            below = sum(
                STENCIL_COEFFS[k] * corner[x, t, 2 * ROWS - k : 3 * ROWS - k, :] for k in range(1, REACH + 1)
            )
            for share, amount, start in (
                (high_share, above, REACH + lay.cy - ROWS),
                (low_share, below, REACH),
            ):
                rows = slice(start, start + ROWS)
                field[planes_start + x, t, rows, :] += s[planes_start + x, t, rows, :] * (amount * share)
            for share, start, cut in (
                (high_share, lay.ey - ROWS, REACH),
                (low_share, 0, 2 * ROWS - REACH),
            ):
                source = [corner[j, t, cut : cut + ROWS, :] for j in range(REACH)]
                from_left = sum(STENCIL_COEFFS[x + REACH - j] * source[j] for j in range(x, REACH))
                from_right = sum(STENCIL_COEFFS[REACH + j - x] * source[j] for j in range(x + 1))
                amount = jnp.where(right, from_right, from_left) * share
                rows = slice(start, start + ROWS)
                field[rows_start + x, t, rows, :] += s[rows_start + x, t, rows, :] * amount


def round_kernel(lay, time, *refs):
    nz, ny = len(lay.z_parities), len(lay.y_parities)
    last = time + 2 == lay.steps
    plan, refs = (refs[0], refs[1:]) if last else (None, refs)
    (wavelet, source_cell, stepped, s, planes, p), refs = refs[:6], refs[6:]
    d_in, refs = refs[: nz * ny], refs[nz * ny :]
    (field, history), refs = refs[:2], refs[2:]
    corner = refs[-1]
    latest = history.at[time + 1]
    if time:
        p = history.at[time - 1]
    gx, column, core = lay.place()
    cell, grid_y = source_cell[0], lay.by * lay.ny
    source_x = cell // (grid_y * lay.depth) - gx * lay.bx
    source_y = cell // lay.depth % grid_y - column * lay.cy
    source_z = cell % lay.depth
    z_sides = [lay.z_side(pz) for pz in lay.z_parities]
    y_sides = [lay.y_side(py) for py in lay.y_parities]
    bx, cy, zt = lay.bx, lay.cy, lay.zt

    def injected(x, rows, y, back):
        values = pltpu.roll(planes[x], LANES - back, 1) if back else planes[x]
        return jnp.where(lane_ids(lay.ey) == 0, values, 0.0)[y : y + rows]

    def add_source(target, speed_rows, x, y, count_x, count_y, amount):
        @pl.when((core == 0) & (x >= 0) & (x < count_x) & (y >= 0) & (y < count_y))
        def _():
            tile, lane = source_z // LANES, source_z % LANES
            shape = (count_y, LANES)
            here = (lax.broadcasted_iota(jnp.int32, shape, 0) == y) & (
                lax.broadcasted_iota(jnp.int32, shape, 1) == lane
            )
            target[x, tile] += jnp.where(here, speed_rows(x, tile) * amount, 0.0)

    corners = [(r, h, u & v) for r, u in z_sides for h, v in y_sides]
    for (right, high, valid), message in zip(corners, d_in):
        add_corner(lay, field, s, message, right, high, valid, corner)
    for x in range(lay.ex):
        field[x, 0] += s[x, 0] * injected(x, lay.ey, 0, lay.steps - 1 - time)
    add_source(field, lambda x, t: s[x, t], source_x + REACH, source_y + REACH, lay.ex, lay.ey, wavelet[time])

    for x in range(bx):
        speed = [s[x + REACH, t, REACH : REACH + cy, :] for t in range(zt)]
        out = advance(lay, field, x + REACH, REACH, cy, [p[x, t] for t in range(zt)], speed)
        out[0] += speed[0] * injected(x + REACH, cy, REACH, lay.steps - 2 - time)
        for t in range(zt):
            latest[x, t] = out[t]
            history[time, x, t] = field[x + REACH, t, REACH : REACH + cy, :]
    add_source(
        latest, lambda x, t: s[x + REACH, t, REACH : REACH + cy, :], source_x, source_y, bx, cy, wavelet[time + 1]
    )

    if last:
        own, theirs = refs[:2]
        kept = [lay.steps - 2, lay.steps - 1, 0]
        for slot in range(1, lay.slots - 1):
            kept.append(jnp.where(core == 0, plan[slot], lay.steps - 1 - plan[lay.slots - 1 - slot]))
        for index, moment in enumerate(kept):
            for x in range(bx):
                for t in range(zt):
                    low, high = history[moment, x, t, 0 : lay.by, :], history[moment, x, t, lay.by : cy, :]
                    own[index, x, t] = jnp.where(core == 0, low, high)
                    theirs[index, x, t] = jnp.where(core == 0, high, low)
    else:
        z_out, y_out, d_out = refs[0], refs[1 : 1 + ny], refs[1 + ny : 1 + ny + nz * ny]
        for x in range(bx):
            store_packed(z_out, x, [latest[x, t] for t in range(zt)], lay, cy)
        for message, (high, _) in zip(y_out, y_sides):
            write_y_message(message, 0, latest, lay, high)
        corners = [(right, high) for right, _ in z_sides for high, _ in y_sides]
        for message, (right, high) in zip(d_out, corners):
            write_d_message(message, latest, lay, right, high)


def finish_kernel(lay, own, theirs, stored, image_before, *outs):
    src_prev, src_now, rec_prev, rec_now, snapshots, image = outs
    _, _, core = lay.place()
    first = core == 0
    for x in range(lay.bx):
        for t in range(lay.zt):
            width = LANES if t + 1 < lay.zt else lay.rest
            lanes = slice(t * LANES, t * LANES + width)
            source = [jnp.where(first, own[i, x, t], theirs[i, x, t])[:, :width] for i in range(lay.slots + 1)]
            receiver = [jnp.where(first, theirs[i, x, t], own[i, x, t])[:, :width] for i in range(lay.slots + 1)]
            src_prev[x, :, lanes], src_now[x, :, lanes] = source[0], source[1]
            rec_prev[x, :, lanes], rec_now[x, :, lanes] = receiver[0], receiver[1]
            total = image_before[x, :, lanes]
            for slot in range(lay.slots):
                kept = source[1] if slot == lay.slots - 1 else source[2 + slot]
                snapshots[slot, x, :, lanes] = kept.astype(jnp.bfloat16)
                crossed = receiver[1] if slot == 0 else receiver[1 + lay.slots - slot]
                total += stored[slot, x, :, lanes].astype(jnp.float32) * crossed
            image[x, :, lanes] = total


def call(kernel, outs, operands, scratch=(), scalars=0, aliases={}, from_hbm=False):
    in_specs = [pl.BlockSpec(memory_space=pltpu.SMEM)] * scalars
    space = pltpu.HBM if from_hbm else pltpu.VMEM
    if from_hbm:
        operands = [pltpu.with_memory_space_constraint(x, pltpu.HBM) for x in operands]
    in_specs += [pl.BlockSpec(memory_space=space)] * (len(operands) - scalars)
    return pl.pallas_call(
        kernel,
        out_shape=[jax.ShapeDtypeStruct(shape, dtype) for shape, dtype in outs],
        in_specs=in_specs,
        out_specs=[pl.BlockSpec(memory_space=pltpu.VMEM)] * len(outs),
        scratch_shapes=list(scratch),
        input_output_aliases=aliases,
        compiler_params=pltpu.CompilerParams(vmem_limit_bytes=6 * 1024 * 1024),
    )(*operands)


def share_in_chip(lay, message):
    other = lax.ppermute(message, AXES, lay.core_permutation())
    message = jnp.concatenate([message, other], 1)[None]
    if message.shape[2] != LANES:
        spare = -message.shape[2] % LANES
        fill = jnp.full((1, lay.trace_rows, spare), -1e6, jnp.float32)
        message = jnp.concatenate([message, fill], 2)
        message = message.reshape(lay.trace_rows, -1, LANES).transpose(1, 0, 2)
    return message


def spread(lay, message):
    for count, move in (
        (lay.columns, lambda x, c, bit: (x, c ^ bit)),
        (lay.nx, lambda x, c, bit: (x ^ bit, c)),
    ):
        assert count & (count - 1) == 0
        bit = 2
        while bit < count:
            pairs = lay.permutation(functools.partial(move, bit=bit))
            message = jnp.concatenate([message, lax.ppermute(message, AXES, pairs)], 0)
            bit *= 2
    return message


def body(
    mesh,
    source_prev,
    source_now,
    receiver_prev,
    receiver_now,
    speed_squared,
    wavelet,
    source_cell,
    traces,
    receiver_cells,
    plan,
    stored_snapshots,
    image_before,
):
    steps, slots = wavelet.shape[0], plan.shape[0]
    lay = Layout(mesh, *source_now.shape, steps, slots)
    f32 = jnp.float32
    first = lax.axis_index("gy") % 2 == 0
    nz, ny = len(lay.z_parities), len(lay.y_parities)

    half = (3, *source_now.shape)
    inputs = [source_now, source_prev, receiver_now, receiver_prev, speed_squared, traces, receiver_cells]
    mine, swapped, message = call(
        functools.partial(load_kernel, lay),
        [(half, f32), (half, f32), ((lay.trace_rows, traces.shape[1]), f32)],
        inputs,
        [
            pltpu.VMEM((4, *source_now.shape), f32),
            pltpu.VMEM(traces.shape, f32),
            pltpu.VMEM(receiver_cells.shape, jnp.int32),
            pltpu.SemaphoreType.DMA((8,)),
        ],
        from_hbm=True,
    )
    swapped = lax.ppermute(swapped, AXES, lay.core_permutation())
    groups = share_in_chip(lay, message)
    groups = spread(lay, groups)

    block = (lay.bx, lay.zt, lay.cy, LANES)
    ext = (lay.ex, lay.zt, lay.ey, LANES)
    field = (lay.bx + 2 * HALO, lay.zt, lay.cy + 2 * HALO, LANES)
    y_rows = lay.zt * ROWS
    z_shape = (lay.bx, lay.zrows, LANES)
    y_shape = (lay.bx, y_rows, LANES)
    d_shape = (REACH // 2, y_rows, LANES)

    def carrying(planes, rows, first):
        more = pl.cdiv(groups.shape[0] * lay.trace_rows, rows) if first else 0
        return (planes + more, rows, LANES), f32

    outs = [(block, f32)] * 3
    outs += [carrying(lay.bx + 2 * REACH, lay.zrows, pz == 0) for pz in lay.z_parities]
    outs += [carrying(3 * lay.bx, y_rows, py == 0) for py in lay.y_parities]
    outs += [carrying(REACH // 2, y_rows, pz + py == 0) for pz in lay.z_parities for py in lay.y_parities]
    made = call(
        functools.partial(prepare_kernel, lay),
        outs,
        [mine, swapped],
    )
    (p, q, s), made = made[:3], made[3:]
    z_out, y_out, d_out = made[:nz], made[nz : nz + ny], made[nz + ny :]
    filled = z_out[:1] + y_out[:1] + d_out[:1]
    if filled:
        filled = call(
            functools.partial(append_kernel, lay),
            [(m.shape, f32) for m in filled],
            [groups, *filled],
            aliases={1 + i: i for i in range(len(filled))},
        )
        z, y, d = lay.by_kind(filled)
        z_out, y_out, d_out = z + z_out[1:], y + y_out[1:], d + d_out[1:]

    for time in range(0, steps, 2):
        begin, end = time == 0, time + 2 == steps
        z_in = [lax.ppermute(m, AXES, lay.z_permutation(pz)) for m, pz in zip(z_out, lay.z_parities)]
        y_in = [lax.ppermute(m, AXES, lay.y_permutation(py)) for m, py in zip(y_out, lay.y_parities)]
        diagonals = [lay.d_permutation(pz, py) for pz in lay.z_parities for py in lay.y_parities]
        d_in = [lax.ppermute(m, AXES, pairs) for m, pairs in zip(d_out, diagonals)]
        made = call(
            functools.partial(side_kernel, lay, time),
            [(ext, f32)] * (2 if begin else 1),
            [p, q, s, *z_in, *y_in],
            [pltpu.VMEM(ext, f32)] * begin + [pltpu.VMEM(field, f32)],
        )
        stepped = made[0]
        if begin:
            s = made[1]
            groups, stepped = lax.optimization_barrier((groups, stepped))
            carried = z_in[:1] + y_in[:1] + d_in[:1]
            (planes,) = call(
                functools.partial(planes_kernel, lay),
                [((lay.ex, lay.ey, LANES), f32)],
                [groups, *carried],
                [pltpu.VMEM((lay.ex * lay.ey, LANES), f32)],
            )
        outs = [(ext, f32), ((steps, *block), f32)]
        if end:
            outs += [((slots + 1, lay.bx, lay.zt, lay.by, LANES), f32)] * 2
        else:
            outs += [(z_shape, f32)] + [(y_shape, f32)] * ny + [(d_shape, f32)] * (nz * ny)
        scalars = [plan] * end + [wavelet, source_cell]
        operands = scalars + [stepped, s, planes, p, *d_in]
        made = call(
            functools.partial(round_kernel, lay, time),
            outs,
            operands,
            [pltpu.VMEM((REACH, lay.zt, 3 * ROWS, LANES), f32)],
            scalars=len(scalars),
            aliases={len(scalars): 0} | ({} if begin else {len(scalars) + 3: 1}),
        )
        q, p = made[:2]
        if end:
            own, theirs = made[2:]
        else:
            z_out = [made[2]] * nz
            y_out, d_out = made[3 : 3 + ny], made[3 + ny :]

    theirs = lax.ppermute(theirs, AXES, lay.core_permutation())
    shape = source_now.shape
    return tuple(
        call(
            functools.partial(finish_kernel, lay),
            [(shape, f32)] * 4 + [(stored_snapshots.shape, jnp.bfloat16), (shape, f32)],
            [own, theirs, stored_snapshots, image_before],
        )
    )


def solution(mesh):
    block = P(("shot", "gx"), "gy", None)
    line = P("shot", ("gx", "gy"))
    volume = P("shot", "gx", "gy", None)
    return jax.shard_map(
        functools.partial(body, mesh),
        mesh=mesh,
        in_specs=(block,) * 5 + (P("shot"), P("shot"), line, line, P("shot"), volume, block),
        out_specs=(block,) * 4 + (volume, block),
        check_vma=False,
    )
```

```python
import functools

import jax
import jax.numpy as jnp
from jax import lax
from jax.experimental import pallas as pl
from jax.experimental.pallas import tpu as pltpu
from jax.sharding import PartitionSpec as P

STENCIL_COEFFS = (-205.0 / 72.0, 8.0 / 5.0, -1.0 / 5.0, 8.0 / 315.0, -1.0 / 560.0)
REACH = 4
HALO = 2 * REACH
LANES = 128
ROWS = 8
AXES = ("gx", "gy")


class Layout:
    def __init__(self, mesh, block_x, block_y, depth, steps, slots):
        self.nx, self.ny = mesh.shape["gx"], mesh.shape["gy"]
        self.columns = self.ny // 2
        self.bx, self.by, self.depth = block_x, block_y, depth
        self.steps, self.slots = steps, slots
        self.cy = 2 * block_y
        self.zt = pl.cdiv(depth + REACH, LANES)
        self.rest = depth - (self.zt - 1) * LANES
        self.packed = 0 < self.rest <= LANES // 2
        self.ex, self.ey = block_x + 2 * REACH, self.cy + 2 * REACH
        self.zrows = self.cy * (self.zt - 1) + self.cy // 2 if self.packed else self.cy * self.zt
        self.trace_rows = pl.cdiv(steps + 2, 2 * ROWS) * 2 * ROWS
        self.z_parities = [p for p in (0, 1) if p + 1 < self.nx]
        self.y_parities = [p for p in (0, 1) if p + 1 < self.columns]
        assert self.ny % 2 == 0 and block_x >= HALO and block_y % ROWS == 0 and steps % 2 == 0

    def device(self, x, column, core):
        return x * self.ny + 2 * column + core

    def permutation(self, move):
        pairs = []
        for x in range(self.nx):
            for column in range(self.columns):
                other = move(x, column)
                there = 0 <= other[0] < self.nx and 0 <= other[1] < self.columns
                for core in (0, 1):
                    target = self.device(*other, core) if there else self.device(x, column, 1 - core)
                    pairs.append((self.device(x, column, core), target))
        return pairs

    def z_permutation(self, pz):
        return self.permutation(lambda x, c: (x + (1 if x % 2 == pz else -1), c))

    def y_permutation(self, py):
        return self.permutation(lambda x, c: (x, c + (1 if c % 2 == py else -1)))

    def d_permutation(self, pz, py):
        return self.permutation(
            lambda x, c: (x + (1 if x % 2 == pz else -1), c + (1 if c % 2 == py else -1))
        )

    def carriers(self, z_messages, y_messages, d_messages):
        starts = (self.bx + 2 * REACH, 3 * self.bx, REACH // 2)
        return [(m, start) for ms, start in zip((z_messages, y_messages, d_messages), starts) for m in ms]

    def by_kind(self, messages):
        z, y = bool(self.z_parities), bool(self.y_parities)
        return messages[:z], messages[z : z + y], messages[z + y :]

    def spot(self, message, start, group, part):
        chunk = group * (self.trace_rows // ROWS) + part
        per_plane = message.shape[1] // ROWS
        return start + chunk // per_plane, chunk % per_plane * ROWS

    def core_permutation(self):
        return self.permutation(lambda x, c: (-1, -1))

    def place(self):
        gx, gy = lax.axis_index("gx"), lax.axis_index("gy")
        return gx, gy // 2, gy % 2

    def z_side(self, pz):
        gx, _, _ = self.place()
        right = gx % 2 == pz
        return right, jnp.where(right, gx + 1 < self.nx, gx > 0)

    def y_side(self, py):
        _, column, _ = self.place()
        high = column % 2 == py
        return high, jnp.where(high, column + 1 < self.columns, column > 0)


def lane_ids(rows):
    return lax.broadcasted_iota(jnp.int32, (rows, LANES), 1)


def pack(tiles, lay, rows):
    if not lay.packed:
        return list(tiles)
    last = tiles[-1]
    return list(tiles[:-1]) + [last[: rows // 2] + pltpu.roll(last[rows // 2 :], LANES // 2, 1)]


def unpack(block, lay, rows):
    tiles = [block[t * rows : (t + 1) * rows] for t in range(lay.zt - 1)]
    start = (lay.zt - 1) * rows
    if not lay.packed:
        return tiles + [block[start : start + rows]]
    both = block[start : start + rows // 2]
    low = lane_ids(rows // 2) < LANES // 2
    first = jnp.where(low, both, 0.0)
    second = pltpu.roll(jnp.where(low, 0.0, both), LANES // 2, 1)
    return tiles + [jnp.concatenate([first, second], 0)]


def store_packed(ref, index, tiles, lay, rows):
    row = 0
    for piece in pack(tiles, lay, rows):
        ref[index, row : row + piece.shape[0], :] = piece
        row += piece.shape[0]


def write_y_message(ref, lead, source, lay, high):
    for x in range(lay.bx):
        for t in range(lay.zt):
            rows = jnp.where(
                high, source[x, t, lay.cy - ROWS : lay.cy, :], source[x, t, 0:ROWS, :]
            )
            ref[lead * lay.bx + x, t * ROWS : (t + 1) * ROWS, :] = rows


def write_d_message(ref, source, lay, right, high):
    start = jnp.where(right, lay.bx - REACH, 0)
    upper = lax.broadcasted_iota(jnp.int32, (ROWS, LANES), 0) < REACH
    for x in range(REACH // 2):
        for t in range(lay.zt):
            a, b = (
                jnp.where(
                    high,
                    source[start + plane, t, lay.cy - ROWS : lay.cy, :],
                    source[start + plane, t, 0:ROWS, :],
                )
                for plane in (x, x + REACH // 2)
            )
            last = jnp.where(upper, pltpu.roll(a, REACH, 0), b)
            first = jnp.where(upper, a, pltpu.roll(b, REACH, 0))
            ref[x, t * ROWS : (t + 1) * ROWS, :] = jnp.where(high, last, first)


def load_kernel(lay, src_now, src_prev, rec_now, rec_prev, speed, traces, cells, mine, swap, message, *scratch):
    held, samples, numbers, semaphores = scratch
    copies = [
        (src_now, held.at[0]),
        (rec_now, held.at[1]),
        (src_prev, held.at[2]),
        (rec_prev, held.at[3]),
        (speed, mine.at[2]),
        (speed, swap.at[2]),
        (traces, samples),
        (cells, numbers),
    ]
    copies = [pltpu.make_async_copy(a, b, semaphores.at[i]) for i, (a, b) in enumerate(copies)]
    for copy in copies:
        copy.start()
    for copy in copies:
        copy.wait()
    _, _, core = lay.place()
    for index in range(2):
        for x in range(lay.bx):
            source, receiver = held[2 * index, x], held[2 * index + 1, x]
            mine[index, x] = jnp.where(core == 0, source, receiver)
            swap[index, x] = jnp.where(core == 0, receiver, source)
    cell = numbers[...].astype(jnp.float32)
    row = jnp.floor((cell + 0.5) * (1.0 / (lay.by * lay.ny)))
    message[...] = jnp.zeros_like(message)
    message[0 : lay.steps, :] = samples[...]
    message[lay.steps : lay.steps + 1, :] = row
    message[lay.steps + 1 : lay.steps + 2, :] = cell - row * (lay.by * lay.ny)


def prepare_kernel(lay, *refs):
    (own, other), refs = refs[:2], refs[2:]
    (p, q, s), refs = refs[:3], refs[3:]
    nz, ny = len(lay.z_parities), len(lay.y_parities)
    z_messages, refs = refs[:nz], refs[nz:]
    y_messages, d_messages = refs[:ny], refs[ny:]
    _, _, core = lay.place()
    first = core == 0
    edge = (lay.zt - 1) * LANES
    for ref in (p, q, s):
        ref[:, lay.zt - 1, :, :] = jnp.zeros((lay.bx, lay.cy, LANES), jnp.float32)
    for index, ref in enumerate((p, q, s)):
        for x in range(lay.bx):
            for t in range(lay.zt):
                width = LANES if t + 1 < lay.zt else lay.rest
                lanes = slice(t * LANES, t * LANES + width)
                mine = own[index, x, :, lanes]
                theirs = other[index, x, :, lanes]
                ref[x, t, 0 : lay.by, 0:width] = jnp.where(first, mine, theirs)
                ref[x, t, lay.by : lay.cy, 0:width] = jnp.where(first, theirs, mine)
    sides = [lay.z_side(pz)[0] for pz in lay.z_parities]
    for x in range(lay.bx):
        tiles = [p[x, t] for t in range(lay.zt)]
        for message in z_messages:
            store_packed(message, x, tiles, lay, lay.cy)
    for message, right in zip(z_messages, sides):
        start = jnp.where(right, lay.bx - REACH, 0)
        for lead, ref in ((0, q), (1, s)):
            for x in range(REACH):
                tiles = [ref[start + x, t] for t in range(lay.zt)]
                store_packed(message, lay.bx + lead * REACH + x, tiles, lay, lay.cy)
    highs = [lay.y_side(py)[0] for py in lay.y_parities]
    for message, high in zip(y_messages, highs):
        for lead, ref in enumerate((p, q, s)):
            write_y_message(message, lead, ref, lay, high)
    corners = [(right, high) for right in sides for high in highs]
    for message, (right, high) in zip(d_messages, corners):
        write_d_message(message, p, lay, right, high)


def append_kernel(lay, *refs):
    groups, messages = refs[0], refs[1 + (len(refs) - 1) // 2 :]
    for message, start in lay.carriers(*lay.by_kind(messages)):
        for group in range(groups.shape[0]):
            for part in range(lay.trace_rows // ROWS):
                plane, row = lay.spot(message, start, group, part)
                message[plane, row : row + ROWS, :] = groups[group, part * ROWS : (part + 1) * ROWS, :]


def extract_kernel(lay, *refs):
    groups, messages, out = refs[1], refs[2:-1], refs[-1]
    count = groups.shape[0]
    out[0:count] = groups[...]
    for index, (message, start) in enumerate(lay.carriers(*lay.by_kind(messages))):
        for group in range(count):
            for part in range(lay.trace_rows // ROWS):
                plane, row = lay.spot(message, start, group, part)
                out[(index + 1) * count + group, part * ROWS : (part + 1) * ROWS, :] = message[plane, row : row + ROWS, :]


def planes_kernel(lay, groups, planes, total):
    gx, column, core = lay.place()
    start_x, start_y = gx * lay.bx - REACH, column * lay.cy - REACH
    cells = lay.ex * lay.ey
    padded = lay.trace_rows
    total[...] = jnp.zeros_like(total)

    def add(values):
        x = values[lay.steps : lay.steps + 1, :].astype(jnp.int32) - start_x
        y = values[lay.steps + 1 : lay.steps + 2, :].astype(jnp.int32) - start_y
        inside = (x >= 0) & (x < lay.ex) & (y >= 0) & (y < lay.ey)
        cell = jnp.where(inside, x * lay.ey + y, -1)
        ids = lax.broadcasted_iota(jnp.int32, (cells, LANES), 0)
        chosen = jnp.where(ids == cell, 1.0, 0.0).astype(jnp.bfloat16)
        high = values.astype(jnp.bfloat16)
        rest = values - high.astype(jnp.float32)
        middle = rest.astype(jnp.bfloat16)
        low = (rest - middle.astype(jnp.float32)).astype(jnp.bfloat16)
        fill = jnp.zeros((LANES - 3 * padded, LANES), jnp.bfloat16)
        parts = jnp.concatenate([high, middle, low, fill], 0)
        total[...] += lax.dot_general(
            chosen, parts, (((1,), (1,)), ((), ())), preferred_element_type=jnp.float32
        )

    def add_group(group, carry):
        add(groups[group])
        return carry

    lax.fori_loop(0, groups.shape[0], add_group, 0, unroll=groups.shape[0] <= 2 * ROWS)
    summed = total[...]
    summed = (
        summed + pltpu.roll(summed, LANES - padded, 1) + pltpu.roll(summed, LANES - 2 * padded, 1)
    )
    summed = jnp.where(core == 1, summed, 0.0)
    planes[...] = summed.reshape(lay.ex, lay.ey, LANES)


def advance(lay, field, x, y, rows, before, speed):
    lane = lane_ids(rows)
    centre = [field[x, t, y : y + rows, :] for t in range(lay.zt)]
    sums = []
    for k in range(1, REACH + 1):
        left = [pltpu.roll(c, k, 1) for c in centre]
        right = [pltpu.roll(c, LANES - k, 1) for c in centre]
        per_tile = []
        for t in range(lay.zt):
            lower = jnp.where(lane < k, left[t - 1], left[t])
            upper = jnp.where(lane < LANES - k, right[t], right[(t + 1) % lay.zt])
            around = field[x - k, t, y : y + rows, :] + field[x + k, t, y : y + rows, :]
            around += field[x, t, y - k : y - k + rows, :] + field[x, t, y + k : y + k + rows, :]
            per_tile.append(around + (lower + upper))
        sums.append(per_tile)
    out = []
    for t in range(lay.zt):
        drive = 3.0 * STENCIL_COEFFS[0] * centre[t]
        for k in range(REACH):
            drive += STENCIL_COEFFS[k + 1] * sums[k][t]
        out.append(2.0 * centre[t] - before[t] + speed[t] * drive)
    return out


def side_kernel(lay, time, *refs):
    nz, ny = len(lay.z_parities), len(lay.y_parities)
    (p, q, s), refs = refs[:3], refs[3:]
    first = time == 0
    if not first:
        p = p.at[time - 1]
    z_in, refs = refs[:nz], refs[nz:]
    y_in, refs = refs[:ny], refs[ny:]
    stepped, buffer = refs[0], refs[-1]
    z_sides = [lay.z_side(pz) for pz in lay.z_parities]
    y_sides = [lay.y_side(py) for py in lay.y_parities]
    bx, cy, zt = lay.bx, lay.cy, lay.zt
    own_x, own_y = HALO, HALO

    buffer[own_x : own_x + bx, :, own_y : own_y + cy, :] = p[...]
    around = ((own_x - REACH, own_x), (own_x + bx, own_x + bx + REACH))
    for low, high in around if ny == 2 else ((own_x - REACH, own_x + bx + REACH),):
        empty = jnp.zeros((high - low, zt, HALO, LANES), jnp.float32)
        buffer[low:high, :, 0:own_y, :] = empty
        buffer[low:high, :, own_y + cy :, :] = empty
    if nz < 2:
        empty = jnp.zeros((own_x, zt, cy, LANES), jnp.float32)
        buffer[0:own_x, :, own_y : own_y + cy, :] = empty
        buffer[own_x + bx :, :, own_y : own_y + cy, :] = empty
    for (right, valid), message in zip(z_sides, z_in):
        start = jnp.where(right, own_x + bx, 0)
        skip = jnp.where(right, 0, bx - HALO)
        for x in range(HALO):
            block = jnp.where(valid, message[skip + x], 0.0)
            for t, tile in enumerate(unpack(block, lay, cy)):
                buffer[start + x, t, own_y : own_y + cy, :] = tile
    for (high, valid), message in zip(y_sides, y_in):
        start = pl.multiple_of(jnp.where(high, own_y + cy, own_y - ROWS), ROWS)
        for x in range(bx):
            for t in range(zt):
                rows = message[x, t * ROWS : (t + 1) * ROWS, :]
                buffer[own_x + x, t, pl.ds(start, ROWS), :] = jnp.where(valid, rows, 0.0)

    if first:
        s_out, q_ext = refs[1:3]
        for lead, own, ext in ((0, q, q_ext), (1, s, s_out)):
            ext[...] = jnp.zeros_like(ext)
            for x in range(bx):
                for t in range(zt):
                    ext[REACH + x, t, REACH : REACH + cy, :] = own[x, t]
            for (right, valid), message in zip(z_sides, z_in):
                start = jnp.where(right, REACH + bx, 0)
                for x in range(REACH):
                    block = jnp.where(valid, message[bx + lead * REACH + x], 0.0)
                    for t, tile in enumerate(unpack(block, lay, cy)):
                        ext[start + x, t, REACH : REACH + cy, :] = tile
            for is_high, start, cut in ((False, 0, ROWS - REACH), (True, REACH + cy, 0)):
                wants = [v & (h if is_high else ~h) for h, v in y_sides]
                for x in range(bx):
                    for t in range(zt):
                        rows = slice(t * ROWS + cut, t * ROWS + cut + REACH)
                        ext[REACH + x, t, start : start + REACH, :] = sum(
                            (jnp.where(w, m[(lead + 1) * bx + x, rows, :], 0.0) for w, m in zip(wants, y_in)),
                            jnp.zeros((REACH, LANES), jnp.float32),
                        )
        q, s = q_ext, s_out

    for x in range(lay.ex):
        inside = REACH <= x < REACH + bx
        y, count = (0, lay.ey) if inside else (REACH, cy)
        out = advance(
            lay, buffer, x + REACH, y + REACH, count,
            [q[x, t, y : y + count, :] for t in range(zt)],
            [s[x, t, y : y + count, :] for t in range(zt)],
        )
        for t in range(zt):
            stepped[x, t, y : y + count, :] = out[t]


def add_corner(lay, field, s, message, right, high, valid, corner):
    empty = jnp.zeros((REACH, lay.zt, ROWS, LANES), jnp.float32)
    corner[:, :, 0:ROWS, :] = empty
    corner[:, :, 2 * ROWS :, :] = empty
    upper = lax.broadcasted_iota(jnp.int32, (ROWS, LANES), 0) < REACH
    near = jnp.where(upper, 1.0, 0.0)
    keep = jnp.where(valid, jnp.where(high, near, 1.0 - near), 0.0)
    for x in range(REACH // 2):
        for t in range(lay.zt):
            rows = message[x, t * ROWS : (t + 1) * ROWS, :]
            turned = pltpu.roll(rows, REACH, 0)
            corner[x, t, ROWS : 2 * ROWS, :] = jnp.where(high, rows, turned) * keep
            corner[x + REACH // 2, t, ROWS : 2 * ROWS, :] = jnp.where(high, turned, rows) * keep
    high_share, low_share = jnp.where(high, 1.0, 0.0), jnp.where(high, 0.0, 1.0)
    planes_start = jnp.where(right, REACH + lay.bx, 0)
    rows_start = jnp.where(right, lay.bx, REACH)
    for x in range(REACH):
        for t in range(lay.zt):
            above = sum(STENCIL_COEFFS[k] * corner[x, t, k : k + ROWS, :] for k in range(1, REACH + 1))
            below = sum(
                STENCIL_COEFFS[k] * corner[x, t, 2 * ROWS - k : 3 * ROWS - k, :] for k in range(1, REACH + 1)
            )
            for share, amount, start in (
                (high_share, above, REACH + lay.cy - ROWS),
                (low_share, below, REACH),
            ):
                rows = slice(start, start + ROWS)
                field[planes_start + x, t, rows, :] += s[planes_start + x, t, rows, :] * (amount * share)
            for share, start, cut in (
                (high_share, lay.ey - ROWS, REACH),
                (low_share, 0, 2 * ROWS - REACH),
            ):
                source = [corner[j, t, cut : cut + ROWS, :] for j in range(REACH)]
                from_left = sum(STENCIL_COEFFS[x + REACH - j] * source[j] for j in range(x, REACH))
                from_right = sum(STENCIL_COEFFS[REACH + j - x] * source[j] for j in range(x + 1))
                amount = jnp.where(right, from_right, from_left) * share
                rows = slice(start, start + ROWS)
                field[rows_start + x, t, rows, :] += s[rows_start + x, t, rows, :] * amount


def round_kernel(lay, time, *refs):
    nz, ny = len(lay.z_parities), len(lay.y_parities)
    last = time + 2 == lay.steps
    (source_cell, plan, wavelet, stepped, s, planes, p), refs = refs[:7], refs[7:]
    d_in, refs = refs[: nz * ny], refs[nz * ny :]
    (field, history), refs = refs[:2], refs[2:]
    corner = refs[-1]
    latest = history.at[time + 1]
    if time:
        p = history.at[time - 1]
    gx, column, core = lay.place()
    cell, grid_y = source_cell[0], lay.by * lay.ny
    source_x = cell // (grid_y * lay.depth) - gx * lay.bx
    source_y = cell // lay.depth % grid_y - column * lay.cy
    source_z = cell % lay.depth
    z_sides = [lay.z_side(pz) for pz in lay.z_parities]
    y_sides = [lay.y_side(py) for py in lay.y_parities]
    bx, cy, zt = lay.bx, lay.cy, lay.zt

    def injected(x, rows, y, back):
        values = pltpu.roll(planes[x], LANES - back, 1) if back else planes[x]
        return jnp.where(lane_ids(lay.ey) == 0, values, 0.0)[y : y + rows]

    def add_source(target, speed_rows, x, y, count_x, count_y, amount):
        @pl.when((core == 0) & (x >= 0) & (x < count_x) & (y >= 0) & (y < count_y))
        def _():
            tile, lane = source_z // LANES, source_z % LANES
            shape = (count_y, LANES)
            here = (lax.broadcasted_iota(jnp.int32, shape, 0) == y) & (
                lax.broadcasted_iota(jnp.int32, shape, 1) == lane
            )
            target[x, tile] += jnp.where(here, speed_rows(x, tile) * amount, 0.0)

    corners = [(r, h, u & v) for r, u in z_sides for h, v in y_sides]
    for (right, high, valid), message in zip(corners, d_in):
        add_corner(lay, field, s, message, right, high, valid, corner)
    for x in range(lay.ex):
        field[x, 0] += s[x, 0] * injected(x, lay.ey, 0, lay.steps - 1 - time)
    add_source(field, lambda x, t: s[x, t], source_x + REACH, source_y + REACH, lay.ex, lay.ey, wavelet[:, time : time + 1])

    for x in range(bx):
        speed = [s[x + REACH, t, REACH : REACH + cy, :] for t in range(zt)]
        out = advance(lay, field, x + REACH, REACH, cy, [p[x, t] for t in range(zt)], speed)
        out[0] += speed[0] * injected(x + REACH, cy, REACH, lay.steps - 2 - time)
        for t in range(zt):
            latest[x, t] = out[t]
            history[time, x, t] = field[x + REACH, t, REACH : REACH + cy, :]
    add_source(
        latest, lambda x, t: s[x + REACH, t, REACH : REACH + cy, :], source_x, source_y, bx, cy, wavelet[:, time + 1 : time + 2]
    )

    if last:
        own, theirs = refs[:2]

        def kept(index, x, t):
            if index < 3:
                return history[(lay.steps - 2, lay.steps - 1, 0)[index], x, t]
            slot = index - 2
            rows = history[slot, x, t]
            for moment in range(slot + 1, lay.steps - lay.slots + slot + 1):
                rows = jnp.where(moments[slot] == moment, history[moment, x, t], rows)
            return rows

        moments = {}
        for slot in range(1, lay.slots - 1):
            mirrored = lay.slots - 1 - slot
            moment = jnp.where(core == 0, plan[:, slot : slot + 1], lay.steps - 1 - plan[:, mirrored : mirrored + 1])
            moments[slot] = jnp.broadcast_to(moment, (cy, LANES))
        for index in range(lay.slots + 1):
            for x in range(bx):
                for t in range(zt):
                    rows = kept(index, x, t)
                    low, high = rows[0 : lay.by], rows[lay.by :]
                    own[index, x, t] = jnp.where(core == 0, low, high)
                    theirs[index, x, t] = jnp.where(core == 0, high, low)
    else:
        z_out, y_out, d_out = refs[0], refs[1 : 1 + ny], refs[1 + ny : 1 + ny + nz * ny]
        for x in range(bx):
            store_packed(z_out, x, [latest[x, t] for t in range(zt)], lay, cy)
        for message, (high, _) in zip(y_out, y_sides):
            write_y_message(message, 0, latest, lay, high)
        corners = [(right, high) for right, _ in z_sides for high, _ in y_sides]
        for message, (right, high) in zip(d_out, corners):
            write_d_message(message, latest, lay, right, high)


def finish_kernel(lay, own, theirs, stored, image_before, *outs):
    src_prev, src_now, rec_prev, rec_now, snapshots, image = outs
    _, _, core = lay.place()
    first = core == 0
    for x in range(lay.bx):
        for t in range(lay.zt):
            width = LANES if t + 1 < lay.zt else lay.rest
            lanes = slice(t * LANES, t * LANES + width)
            source = [jnp.where(first, own[i, x, t], theirs[i, x, t])[:, :width] for i in range(lay.slots + 1)]
            receiver = [jnp.where(first, theirs[i, x, t], own[i, x, t])[:, :width] for i in range(lay.slots + 1)]
            src_prev[x, :, lanes], src_now[x, :, lanes] = source[0], source[1]
            rec_prev[x, :, lanes], rec_now[x, :, lanes] = receiver[0], receiver[1]
            total = image_before[x, :, lanes]
            for slot in range(lay.slots):
                kept = source[1] if slot == lay.slots - 1 else source[2 + slot]
                snapshots[slot, x, :, lanes] = kept.astype(jnp.bfloat16)
                crossed = receiver[1] if slot == 0 else receiver[1 + lay.slots - slot]
                total += stored[slot, x, :, lanes].astype(jnp.float32) * crossed
            image[x, :, lanes] = total


def call(kernel, outs, operands, scratch=(), scalars=0, aliases={}, from_hbm=False):
    in_specs = [pl.BlockSpec(memory_space=pltpu.SMEM)] * scalars
    space = pltpu.HBM if from_hbm else pltpu.VMEM
    if from_hbm:
        operands = [pltpu.with_memory_space_constraint(x, pltpu.HBM) for x in operands]
    in_specs += [pl.BlockSpec(memory_space=space)] * (len(operands) - scalars)
    return pl.pallas_call(
        kernel,
        out_shape=[jax.ShapeDtypeStruct(shape, dtype) for shape, dtype in outs],
        in_specs=in_specs,
        out_specs=[pl.BlockSpec(memory_space=pltpu.VMEM)] * len(outs),
        scratch_shapes=list(scratch),
        input_output_aliases=aliases,
        compiler_params=pltpu.CompilerParams(vmem_limit_bytes=6 * 1024 * 1024),
    )(*operands)


def share_in_chip(lay, message):
    other = lax.ppermute(message, AXES, lay.core_permutation())
    message = jnp.concatenate([message, other], 1)[None]
    if message.shape[2] != LANES:
        spare = -message.shape[2] % LANES
        fill = jnp.full((1, lay.trace_rows, spare), -1e6, jnp.float32)
        message = jnp.concatenate([message, fill], 2)
        message = message.reshape(lay.trace_rows, -1, LANES).transpose(1, 0, 2)
    return message


def spread(lay, message):
    for count, move in (
        (lay.columns, lambda x, c, bit: (x, c ^ bit)),
        (lay.nx, lambda x, c, bit: (x ^ bit, c)),
    ):
        assert count & (count - 1) == 0
        bit = 2
        while bit < count:
            pairs = lay.permutation(functools.partial(move, bit=bit))
            message = jnp.concatenate([message, lax.ppermute(message, AXES, pairs)], 0)
            bit *= 2
    return message


def body(
    mesh,
    source_prev,
    source_now,
    receiver_prev,
    receiver_now,
    speed_squared,
    wavelet,
    source_cell,
    traces,
    receiver_cells,
    plan,
    stored_snapshots,
    image_before,
):
    steps, slots = wavelet.shape[0], plan.shape[0]
    lay = Layout(mesh, *source_now.shape, steps, slots)
    f32 = jnp.float32
    first = lax.axis_index("gy") % 2 == 0
    nz, ny = len(lay.z_parities), len(lay.y_parities)

    half = (3, *source_now.shape)
    inputs = [source_now, source_prev, receiver_now, receiver_prev, speed_squared, traces, receiver_cells]
    mine, swapped, message = call(
        functools.partial(load_kernel, lay),
        [(half, f32), (half, f32), ((lay.trace_rows, traces.shape[1]), f32)],
        inputs,
        [
            pltpu.VMEM((4, *source_now.shape), f32),
            pltpu.VMEM(traces.shape, f32),
            pltpu.VMEM(receiver_cells.shape, jnp.int32),
            pltpu.SemaphoreType.DMA((8,)),
        ],
        from_hbm=True,
    )
    swapped = lax.ppermute(swapped, AXES, lay.core_permutation())
    groups = share_in_chip(lay, message)
    block = (lay.bx, lay.zt, lay.cy, LANES)
    ext = (lay.ex, lay.zt, lay.ey, LANES)
    field = (lay.bx + 2 * HALO, lay.zt, lay.cy + 2 * HALO, LANES)
    y_rows = lay.zt * ROWS
    z_shape = (lay.bx, lay.zrows, LANES)
    y_shape = (lay.bx, y_rows, LANES)
    d_shape = (REACH // 2, y_rows, LANES)

    def carrying(planes, rows, first):
        more = pl.cdiv(groups.shape[0] * lay.trace_rows, rows) if first else 0
        return (planes + more, rows, LANES), f32

    outs = [(block, f32)] * 3
    outs += [carrying(lay.bx + 2 * REACH, lay.zrows, pz == 0) for pz in lay.z_parities]
    outs += [carrying(3 * lay.bx, y_rows, py == 0) for py in lay.y_parities]
    outs += [carrying(REACH // 2, y_rows, pz + py == 0) for pz in lay.z_parities for py in lay.y_parities]
    made = call(
        functools.partial(prepare_kernel, lay),
        outs,
        [mine, swapped],
    )
    (p, q, s), made = made[:3], made[3:]
    z_out, y_out, d_out = made[:nz], made[nz : nz + ny], made[nz + ny :]
    filled = z_out[:1] + y_out[:1] + d_out[:1]
    if filled:
        filled = call(
            functools.partial(append_kernel, lay),
            [(m.shape, f32) for m in filled],
            [groups, *filled],
            aliases={1 + i: i for i in range(len(filled))},
        )
        z, y, d = lay.by_kind(filled)
        z_out, y_out, d_out = z + z_out[1:], y + y_out[1:], d + d_out[1:]

    for time in range(0, steps, 2):
        begin, end = time == 0, time + 2 == steps
        z_in = [lax.ppermute(m, AXES, lay.z_permutation(pz)) for m, pz in zip(z_out, lay.z_parities)]
        y_in = [lax.ppermute(m, AXES, lay.y_permutation(py)) for m, py in zip(y_out, lay.y_parities)]
        diagonals = [lay.d_permutation(pz, py) for pz in lay.z_parities for py in lay.y_parities]
        d_in = [lax.ppermute(m, AXES, pairs) for m, pairs in zip(d_out, diagonals)]
        if begin:
            d_in = list(lax.optimization_barrier(tuple(d_in)))
            carried = z_in[:1] + y_in[:1] + d_in[:1]
            (gathered,) = call(
                functools.partial(extract_kernel, lay),
                [((groups.shape[0] * (1 + len(carried)), *groups.shape[1:]), f32)],
                [source_cell, groups, *carried],
                scalars=1,
            )
            gathered = spread(lay, gathered)
        made = call(
            functools.partial(side_kernel, lay, time),
            [(ext, f32)] * (2 if begin else 1),
            [p, q, s, *z_in, *y_in],
            [pltpu.VMEM(ext, f32)] * begin + [pltpu.VMEM(field, f32)],
        )
        stepped = made[0]
        if begin:
            s = made[1]
            gathered, stepped = lax.optimization_barrier((gathered, stepped))
            (planes,) = call(
                functools.partial(planes_kernel, lay),
                [((lay.ex, lay.ey, LANES), f32)],
                [gathered],
                [pltpu.VMEM((lay.ex * lay.ey, LANES), f32)],
            )
        outs = [(ext, f32), ((steps, *block), f32)]
        if end:
            outs += [((slots + 1, lay.bx, lay.zt, lay.by, LANES), f32)] * 2
        else:
            outs += [(z_shape, f32)] + [(y_shape, f32)] * ny + [(d_shape, f32)] * (nz * ny)
        made = call(
            functools.partial(round_kernel, lay, time),
            outs,
            [source_cell, plan[None], wavelet[None], stepped, s, planes, p, *d_in],
            [pltpu.VMEM((REACH, lay.zt, 3 * ROWS, LANES), f32)],
            scalars=1,
            aliases={3: 0} | ({} if begin else {6: 1}),
        )
        q, p = made[:2]
        if end:
            own, theirs = made[2:]
        else:
            z_out = [made[2]] * nz
            y_out, d_out = made[3 : 3 + ny], made[3 + ny :]

    theirs = lax.ppermute(theirs, AXES, lay.core_permutation())
    shape = source_now.shape
    return tuple(
        call(
            functools.partial(finish_kernel, lay),
            [(shape, f32)] * 4 + [(stored_snapshots.shape, jnp.bfloat16), (shape, f32)],
            [own, theirs, stored_snapshots, image_before],
        )
    )


def solution(mesh):
    block = P(("shot", "gx"), "gy", None)
    line = P("shot", ("gx", "gy"))
    volume = P("shot", "gx", "gy", None)
    return jax.shard_map(
        functools.partial(body, mesh),
        mesh=mesh,
        in_specs=(block,) * 5 + (P("shot"), P("shot"), line, line, P("shot"), volume, block),
        out_specs=(block,) * 4 + (volume, block),
        check_vma=False,
    )
```

```python
import functools

import jax
import jax.numpy as jnp
from jax import lax
from jax.experimental import pallas as pl
from jax.experimental.pallas import tpu as pltpu
from jax.sharding import PartitionSpec as P

STENCIL_COEFFS = (-205.0 / 72.0, 8.0 / 5.0, -1.0 / 5.0, 8.0 / 315.0, -1.0 / 560.0)
REACH = 4
HALO = 2 * REACH
LANES = 128
ROWS = 8
AXES = ("gx", "gy")


class Layout:
    def __init__(self, mesh, block_x, block_y, depth, steps, slots):
        self.nx, self.ny = mesh.shape["gx"], mesh.shape["gy"]
        self.columns = self.ny // 2
        self.bx, self.by, self.depth = block_x, block_y, depth
        self.steps, self.slots = steps, slots
        self.cy = 2 * block_y
        self.zt = pl.cdiv(depth + REACH, LANES)
        self.rest = depth - (self.zt - 1) * LANES
        self.packed = 0 < self.rest <= LANES // 2
        self.ex, self.ey = block_x + 2 * REACH, self.cy + 2 * REACH
        self.zrows = self.cy * (self.zt - 1) + self.cy // 2 if self.packed else self.cy * self.zt
        self.trace_rows = pl.cdiv(steps + 2, 2 * ROWS) * 2 * ROWS
        self.z_parities = [p for p in (0, 1) if p + 1 < self.nx]
        self.y_parities = [p for p in (0, 1) if p + 1 < self.columns]
        assert self.ny % 2 == 0 and block_x >= HALO and block_x % 2 == 0 and block_y % ROWS == 0 and steps % 2 == 0

    def device(self, x, column, core):
        return x * self.ny + 2 * column + core

    def permutation(self, move):
        pairs = []
        for x in range(self.nx):
            for column in range(self.columns):
                other = move(x, column)
                there = 0 <= other[0] < self.nx and 0 <= other[1] < self.columns
                for core in (0, 1):
                    target = self.device(*other, core) if there else self.device(x, column, 1 - core)
                    pairs.append((self.device(x, column, core), target))
        return pairs

    def z_permutation(self, pz):
        return self.permutation(lambda x, c: (x + (1 if x % 2 == pz else -1), c))

    def y_permutation(self, py):
        return self.permutation(lambda x, c: (x, c + (1 if c % 2 == py else -1)))

    def d_permutation(self, pz, py):
        return self.permutation(
            lambda x, c: (x + (1 if x % 2 == pz else -1), c + (1 if c % 2 == py else -1))
        )

    def carriers(self, z_messages, y_messages, d_messages):
        starts = (self.bx + 2 * REACH, 2 * (self.bx // 2), REACH // 2)
        return [(m, start) for ms, start in zip((z_messages, y_messages, d_messages), starts) for m in ms]

    def by_kind(self, messages):
        z, y = bool(self.z_parities), bool(self.y_parities)
        return messages[:z], messages[z : z + y], messages[z + y :]

    def spot(self, message, start, group, part):
        chunk = group * (self.trace_rows // ROWS) + part
        per_plane = message.shape[1] // ROWS
        return start + chunk // per_plane, chunk % per_plane * ROWS

    def core_permutation(self):
        return self.permutation(lambda x, c: (-1, -1))

    def place(self):
        gx, gy = lax.axis_index("gx"), lax.axis_index("gy")
        return gx, gy // 2, gy % 2

    def z_side(self, pz):
        gx, _, _ = self.place()
        right = gx % 2 == pz
        return right, jnp.where(right, gx + 1 < self.nx, gx > 0)

    def y_side(self, py):
        _, column, _ = self.place()
        high = column % 2 == py
        return high, jnp.where(high, column + 1 < self.columns, column > 0)


def lane_ids(rows):
    return lax.broadcasted_iota(jnp.int32, (rows, LANES), 1)


def pack(tiles, lay, rows):
    if not lay.packed:
        return list(tiles)
    last = tiles[-1]
    return list(tiles[:-1]) + [last[: rows // 2] + pltpu.roll(last[rows // 2 :], LANES // 2, 1)]


def unpack(block, lay, rows):
    tiles = [block[t * rows : (t + 1) * rows] for t in range(lay.zt - 1)]
    start = (lay.zt - 1) * rows
    if not lay.packed:
        return tiles + [block[start : start + rows]]
    both = block[start : start + rows // 2]
    low = lane_ids(rows // 2) < LANES // 2
    first = jnp.where(low, both, 0.0)
    second = pltpu.roll(jnp.where(low, 0.0, both), LANES // 2, 1)
    return tiles + [jnp.concatenate([first, second], 0)]


def store_packed(ref, index, tiles, lay, rows):
    row = 0
    for piece in pack(tiles, lay, rows):
        ref[index, row : row + piece.shape[0], :] = piece
        row += piece.shape[0]


def y_rows_of(source, lay, high):
    def rows(plane, t):
        return jnp.where(high, source[plane, t, lay.cy - ROWS : lay.cy, :], source[plane, t, 0:ROWS, :])

    return rows


def y_halves_of(first, second, lay, high):
    upper = lax.broadcasted_iota(jnp.int32, (ROWS, LANES), 0) < REACH
    a, b = y_rows_of(first, lay, high), y_rows_of(second, lay, high)

    def rows(plane, t):
        one, two = a(plane, t), b(plane, t)
        one = jnp.where(high, pltpu.roll(one, REACH, 0), one)
        two = jnp.where(high, two, pltpu.roll(two, REACH, 0))
        return jnp.where(upper, one, two)

    return rows


def write_y_message(ref, lead, rows_of, lay):
    half = lay.bx // 2
    for x in range(half):
        row = 0
        for t in range(lay.zt):
            a, b = rows_of(x, t), rows_of(x + half, t)
            both = [a + pltpu.roll(b, LANES // 2, 1)] if lay.packed and t + 1 == lay.zt else [a, b]
            for rows in both:
                ref[lead * half + x, row : row + ROWS, :] = rows
                row += ROWS


def read_y_message(ref, lead, lay, x, t):
    half = lay.bx // 2
    plane, second = lead * half + x % half, x >= half
    row = 2 * t * ROWS
    if not lay.packed or t + 1 < lay.zt:
        row += ROWS * second
        return ref[plane, row : row + ROWS, :]
    both = ref[plane, row : row + ROWS, :]
    low = lane_ids(ROWS) < LANES // 2
    return pltpu.roll(jnp.where(low, 0.0, both), LANES // 2, 1) if second else jnp.where(low, both, 0.0)


def write_d_message(ref, source, lay, right, high):
    start = jnp.where(right, lay.bx - REACH, 0)
    upper = lax.broadcasted_iota(jnp.int32, (ROWS, LANES), 0) < REACH
    for x in range(REACH // 2):
        for t in range(lay.zt):
            a, b = (
                jnp.where(
                    high,
                    source[start + plane, t, lay.cy - ROWS : lay.cy, :],
                    source[start + plane, t, 0:ROWS, :],
                )
                for plane in (x, x + REACH // 2)
            )
            last = jnp.where(upper, pltpu.roll(a, REACH, 0), b)
            first = jnp.where(upper, a, pltpu.roll(b, REACH, 0))
            ref[x, t * ROWS : (t + 1) * ROWS, :] = jnp.where(high, last, first)


def load_kernel(lay, src_now, src_prev, rec_now, rec_prev, speed, traces, cells, mine, swap, message, *scratch):
    held, samples, numbers, semaphores = scratch
    copies = [
        (src_now, held.at[0]),
        (rec_now, held.at[1]),
        (src_prev, held.at[2]),
        (rec_prev, held.at[3]),
        (speed, mine.at[2]),
        (speed, swap.at[2]),
        (traces, samples),
        (cells, numbers),
    ]
    copies = [pltpu.make_async_copy(a, b, semaphores.at[i]) for i, (a, b) in enumerate(copies)]
    for copy in copies:
        copy.start()
    for copy in copies:
        copy.wait()
    _, _, core = lay.place()
    for index in range(2):
        for x in range(lay.bx):
            source, receiver = held[2 * index, x], held[2 * index + 1, x]
            mine[index, x] = jnp.where(core == 0, source, receiver)
            swap[index, x] = jnp.where(core == 0, receiver, source)
    cell = numbers[...].astype(jnp.float32)
    row = jnp.floor((cell + 0.5) * (1.0 / (lay.by * lay.ny)))
    message[...] = jnp.zeros_like(message)
    message[0 : lay.steps, :] = samples[...]
    message[lay.steps : lay.steps + 1, :] = row
    message[lay.steps + 1 : lay.steps + 2, :] = cell - row * (lay.by * lay.ny)


def prepare_kernel(lay, *refs):
    (own, other, groups), refs = refs[:3], refs[3:]
    (p, q, s), refs = refs[:3], refs[3:]
    nz, ny = len(lay.z_parities), len(lay.y_parities)
    z_messages, refs = refs[:nz], refs[nz:]
    y_messages, d_messages = refs[:ny], refs[ny:]
    _, _, core = lay.place()
    first = core == 0
    edge = (lay.zt - 1) * LANES
    for ref in (p, q, s):
        ref[:, lay.zt - 1, :, :] = jnp.zeros((lay.bx, lay.cy, LANES), jnp.float32)
    for index, ref in enumerate((p, q, s)):
        for x in range(lay.bx):
            for t in range(lay.zt):
                width = LANES if t + 1 < lay.zt else lay.rest
                lanes = slice(t * LANES, t * LANES + width)
                mine = own[index, x, :, lanes]
                theirs = other[index, x, :, lanes]
                ref[x, t, 0 : lay.by, 0:width] = jnp.where(first, mine, theirs)
                ref[x, t, lay.by : lay.cy, 0:width] = jnp.where(first, theirs, mine)
    sides = [lay.z_side(pz)[0] for pz in lay.z_parities]
    for x in range(lay.bx):
        tiles = [p[x, t] for t in range(lay.zt)]
        for message in z_messages:
            store_packed(message, x, tiles, lay, lay.cy)
    for message, right in zip(z_messages, sides):
        start = jnp.where(right, lay.bx - REACH, 0)
        for lead, ref in ((0, q), (1, s)):
            for x in range(REACH):
                tiles = [ref[start + x, t] for t in range(lay.zt)]
                store_packed(message, lay.bx + lead * REACH + x, tiles, lay, lay.cy)
    highs = [lay.y_side(py)[0] for py in lay.y_parities]
    for message, high in zip(y_messages, highs):
        write_y_message(message, 0, y_rows_of(p, lay, high), lay)
        write_y_message(message, 1, y_halves_of(q, s, lay, high), lay)
    corners = [(right, high) for right in sides for high in highs]
    for message, (right, high) in zip(d_messages, corners):
        write_d_message(message, p, lay, right, high)
    for message, start in lay.carriers(z_messages[:1], y_messages[:1], d_messages[:1]):
        for group in range(groups.shape[0]):
            for part in range(lay.trace_rows // ROWS):
                plane, row = lay.spot(message, start, group, part)
                message[plane, row : row + ROWS, :] = groups[group, part * ROWS : (part + 1) * ROWS, :]


def extract_kernel(lay, *refs):
    groups, messages, out = refs[1], refs[2:-1], refs[-1]
    count = groups.shape[0]
    out[0:count] = groups[...]
    for index, (message, start) in enumerate(lay.carriers(*lay.by_kind(messages))):
        for group in range(count):
            for part in range(lay.trace_rows // ROWS):
                plane, row = lay.spot(message, start, group, part)
                out[(index + 1) * count + group, part * ROWS : (part + 1) * ROWS, :] = message[plane, row : row + ROWS, :]


def planes_kernel(lay, groups, planes, total):
    gx, column, core = lay.place()
    start_x, start_y = gx * lay.bx - REACH, column * lay.cy - REACH
    cells = lay.ex * lay.ey
    padded = lay.trace_rows
    total[...] = jnp.zeros_like(total)

    def add(values):
        x = values[lay.steps : lay.steps + 1, :].astype(jnp.int32) - start_x
        y = values[lay.steps + 1 : lay.steps + 2, :].astype(jnp.int32) - start_y
        inside = (x >= 0) & (x < lay.ex) & (y >= 0) & (y < lay.ey)
        cell = jnp.where(inside, x * lay.ey + y, -1)
        ids = lax.broadcasted_iota(jnp.int32, (cells, LANES), 0)
        chosen = jnp.where(ids == cell, 1.0, 0.0).astype(jnp.bfloat16)
        high = values.astype(jnp.bfloat16)
        rest = values - high.astype(jnp.float32)
        middle = rest.astype(jnp.bfloat16)
        low = (rest - middle.astype(jnp.float32)).astype(jnp.bfloat16)
        fill = jnp.zeros((LANES - 3 * padded, LANES), jnp.bfloat16)
        parts = jnp.concatenate([high, middle, low, fill], 0)
        total[...] += lax.dot_general(
            chosen, parts, (((1,), (1,)), ((), ())), preferred_element_type=jnp.float32
        )

    def add_group(group, carry):
        add(groups[group])
        return carry

    lax.fori_loop(0, groups.shape[0], add_group, 0, unroll=groups.shape[0] <= 2 * ROWS)
    summed = total[...]
    summed = (
        summed + pltpu.roll(summed, LANES - padded, 1) + pltpu.roll(summed, LANES - 2 * padded, 1)
    )
    summed = jnp.where(core == 1, summed, 0.0)
    planes[...] = summed.reshape(lay.ex, lay.ey, LANES)


def advance(lay, field, x, y, rows, before, speed):
    lane = lane_ids(rows)
    centre = [field[x, t, y : y + rows, :] for t in range(lay.zt)]
    sums = []
    for k in range(1, REACH + 1):
        left = [pltpu.roll(c, k, 1) for c in centre]
        right = [pltpu.roll(c, LANES - k, 1) for c in centre]
        per_tile = []
        for t in range(lay.zt):
            lower = jnp.where(lane < k, left[t - 1], left[t])
            upper = jnp.where(lane < LANES - k, right[t], right[(t + 1) % lay.zt])
            around = field[x - k, t, y : y + rows, :] + field[x + k, t, y : y + rows, :]
            around += field[x, t, y - k : y - k + rows, :] + field[x, t, y + k : y + k + rows, :]
            per_tile.append(around + (lower + upper))
        sums.append(per_tile)
    out = []
    for t in range(lay.zt):
        drive = 3.0 * STENCIL_COEFFS[0] * centre[t]
        for k in range(REACH):
            drive += STENCIL_COEFFS[k + 1] * sums[k][t]
        out.append(2.0 * centre[t] - before[t] + speed[t] * drive)
    return out


def side_kernel(lay, time, *refs):
    nz, ny = len(lay.z_parities), len(lay.y_parities)
    (p, q, s), refs = refs[:3], refs[3:]
    first = time == 0
    if not first:
        p = p.at[time - 1]
    z_in, refs = refs[:nz], refs[nz:]
    y_in, refs = refs[:ny], refs[ny:]
    stepped, buffer = refs[0], refs[-1]
    z_sides = [lay.z_side(pz) for pz in lay.z_parities]
    y_sides = [lay.y_side(py) for py in lay.y_parities]
    bx, cy, zt = lay.bx, lay.cy, lay.zt
    own_x, own_y = HALO, HALO

    buffer[own_x : own_x + bx, :, own_y : own_y + cy, :] = p[...]
    around = ((own_x - REACH, own_x), (own_x + bx, own_x + bx + REACH))
    for low, high in around if ny == 2 else ((own_x - REACH, own_x + bx + REACH),):
        empty = jnp.zeros((high - low, zt, HALO, LANES), jnp.float32)
        buffer[low:high, :, 0:own_y, :] = empty
        buffer[low:high, :, own_y + cy :, :] = empty
    if nz < 2:
        empty = jnp.zeros((own_x, zt, cy, LANES), jnp.float32)
        buffer[0:own_x, :, own_y : own_y + cy, :] = empty
        buffer[own_x + bx :, :, own_y : own_y + cy, :] = empty
    for (right, valid), message in zip(z_sides, z_in):
        start = jnp.where(right, own_x + bx, 0)
        skip = jnp.where(right, 0, bx - HALO)
        for x in range(HALO):
            block = jnp.where(valid, message[skip + x], 0.0)
            for t, tile in enumerate(unpack(block, lay, cy)):
                buffer[start + x, t, own_y : own_y + cy, :] = tile
    for (high, valid), message in zip(y_sides, y_in):
        start = pl.multiple_of(jnp.where(high, own_y + cy, own_y - ROWS), ROWS)
        for x in range(bx):
            for t in range(zt):
                rows = read_y_message(message, 0, lay, x, t)
                buffer[own_x + x, t, pl.ds(start, ROWS), :] = jnp.where(valid, rows, 0.0)

    if first:
        s_out, q_ext = refs[1:3]
        for lead, own, ext in ((0, q, q_ext), (1, s, s_out)):
            ext[...] = jnp.zeros_like(ext)
            for x in range(bx):
                for t in range(zt):
                    ext[REACH + x, t, REACH : REACH + cy, :] = own[x, t]
            for (right, valid), message in zip(z_sides, z_in):
                start = jnp.where(right, REACH + bx, 0)
                for x in range(REACH):
                    block = jnp.where(valid, message[bx + lead * REACH + x], 0.0)
                    for t, tile in enumerate(unpack(block, lay, cy)):
                        ext[start + x, t, REACH : REACH + cy, :] = tile
            cut = lead * REACH
            for is_high, start in ((False, 0), (True, REACH + cy)):
                wants = [v & (h if is_high else ~h) for h, v in y_sides]
                for x in range(bx):
                    for t in range(zt):
                        rows = sum(
                            (jnp.where(w, read_y_message(m, 1, lay, x, t), 0.0) for w, m in zip(wants, y_in)),
                            jnp.zeros((ROWS, LANES), jnp.float32),
                        )
                        ext[REACH + x, t, start : start + REACH, :] = rows[cut : cut + REACH]
        q, s = q_ext, s_out

    for x in range(lay.ex):
        inside = REACH <= x < REACH + bx
        y, count = (0, lay.ey) if inside else (REACH, cy)
        out = advance(
            lay, buffer, x + REACH, y + REACH, count,
            [q[x, t, y : y + count, :] for t in range(zt)],
            [s[x, t, y : y + count, :] for t in range(zt)],
        )
        for t in range(zt):
            stepped[x, t, y : y + count, :] = out[t]


def add_corner(lay, field, s, message, right, high, valid, corner):
    empty = jnp.zeros((REACH, lay.zt, ROWS, LANES), jnp.float32)
    corner[:, :, 0:ROWS, :] = empty
    corner[:, :, 2 * ROWS :, :] = empty
    upper = lax.broadcasted_iota(jnp.int32, (ROWS, LANES), 0) < REACH
    near = jnp.where(upper, 1.0, 0.0)
    keep = jnp.where(valid, jnp.where(high, near, 1.0 - near), 0.0)
    for x in range(REACH // 2):
        for t in range(lay.zt):
            rows = message[x, t * ROWS : (t + 1) * ROWS, :]
            turned = pltpu.roll(rows, REACH, 0)
            corner[x, t, ROWS : 2 * ROWS, :] = jnp.where(high, rows, turned) * keep
            corner[x + REACH // 2, t, ROWS : 2 * ROWS, :] = jnp.where(high, turned, rows) * keep
    high_share, low_share = jnp.where(high, 1.0, 0.0), jnp.where(high, 0.0, 1.0)
    planes_start = jnp.where(right, REACH + lay.bx, 0)
    rows_start = jnp.where(right, lay.bx, REACH)
    for x in range(REACH):
        for t in range(lay.zt):
            above = sum(STENCIL_COEFFS[k] * corner[x, t, k : k + ROWS, :] for k in range(1, REACH + 1))
            below = sum(
                STENCIL_COEFFS[k] * corner[x, t, 2 * ROWS - k : 3 * ROWS - k, :] for k in range(1, REACH + 1)
            )
            for share, amount, start in (
                (high_share, above, REACH + lay.cy - ROWS),
                (low_share, below, REACH),
            ):
                rows = slice(start, start + ROWS)
                field[planes_start + x, t, rows, :] += s[planes_start + x, t, rows, :] * (amount * share)
            for share, start, cut in (
                (high_share, lay.ey - ROWS, REACH),
                (low_share, 0, 2 * ROWS - REACH),
            ):
                source = [corner[j, t, cut : cut + ROWS, :] for j in range(REACH)]
                from_left = sum(STENCIL_COEFFS[x + REACH - j] * source[j] for j in range(x, REACH))
                from_right = sum(STENCIL_COEFFS[REACH + j - x] * source[j] for j in range(x + 1))
                amount = jnp.where(right, from_right, from_left) * share
                rows = slice(start, start + ROWS)
                field[rows_start + x, t, rows, :] += s[rows_start + x, t, rows, :] * amount


def round_kernel(lay, time, *refs):
    nz, ny = len(lay.z_parities), len(lay.y_parities)
    last = time + 2 == lay.steps
    (source_cell, plan, wavelet, stepped, s, planes, p), refs = refs[:7], refs[7:]
    d_in, refs = refs[: nz * ny], refs[nz * ny :]
    (field, history), refs = refs[:2], refs[2:]
    corner = refs[-1]
    latest = history.at[time + 1]
    if time:
        p = history.at[time - 1]
    gx, column, core = lay.place()
    cell, grid_y = source_cell[0], lay.by * lay.ny
    source_x = cell // (grid_y * lay.depth) - gx * lay.bx
    source_y = cell // lay.depth % grid_y - column * lay.cy
    source_z = cell % lay.depth
    z_sides = [lay.z_side(pz) for pz in lay.z_parities]
    y_sides = [lay.y_side(py) for py in lay.y_parities]
    bx, cy, zt = lay.bx, lay.cy, lay.zt

    def injected(x, rows, y, back):
        values = pltpu.roll(planes[x], LANES - back, 1) if back else planes[x]
        return jnp.where(lane_ids(lay.ey) == 0, values, 0.0)[y : y + rows]

    def add_source(target, speed_rows, x, y, count_x, count_y, amount):
        @pl.when((core == 0) & (x >= 0) & (x < count_x) & (y >= 0) & (y < count_y))
        def _():
            tile, lane = source_z // LANES, source_z % LANES
            shape = (count_y, LANES)
            here = (lax.broadcasted_iota(jnp.int32, shape, 0) == y) & (
                lax.broadcasted_iota(jnp.int32, shape, 1) == lane
            )
            target[x, tile] += jnp.where(here, speed_rows(x, tile) * amount, 0.0)

    corners = [(r, h, u & v) for r, u in z_sides for h, v in y_sides]
    for (right, high, valid), message in zip(corners, d_in):
        add_corner(lay, field, s, message, right, high, valid, corner)
    for x in range(lay.ex):
        field[x, 0] += s[x, 0] * injected(x, lay.ey, 0, lay.steps - 1 - time)
    add_source(field, lambda x, t: s[x, t], source_x + REACH, source_y + REACH, lay.ex, lay.ey, wavelet[:, time : time + 1])

    for x in range(bx):
        speed = [s[x + REACH, t, REACH : REACH + cy, :] for t in range(zt)]
        out = advance(lay, field, x + REACH, REACH, cy, [p[x, t] for t in range(zt)], speed)
        out[0] += speed[0] * injected(x + REACH, cy, REACH, lay.steps - 2 - time)
        for t in range(zt):
            latest[x, t] = out[t]
            history[time, x, t] = field[x + REACH, t, REACH : REACH + cy, :]
    add_source(
        latest, lambda x, t: s[x + REACH, t, REACH : REACH + cy, :], source_x, source_y, bx, cy, wavelet[:, time + 1 : time + 2]
    )

    if last:
        own, theirs = refs[:2]

        def kept(index, x, t):
            if index < 3:
                return history[(lay.steps - 2, lay.steps - 1, 0)[index], x, t]
            slot = index - 2
            rows = history[slot, x, t]
            for moment in range(slot + 1, lay.steps - lay.slots + slot + 1):
                rows = jnp.where(moments[slot] == moment, history[moment, x, t], rows)
            return rows

        moments = {}
        for slot in range(1, lay.slots - 1):
            mirrored = lay.slots - 1 - slot
            moment = jnp.where(core == 0, plan[:, slot : slot + 1], lay.steps - 1 - plan[:, mirrored : mirrored + 1])
            moments[slot] = jnp.broadcast_to(moment, (cy, LANES))
        for index in range(lay.slots + 1):
            for x in range(bx):
                for t in range(zt):
                    rows = kept(index, x, t)
                    low, high = rows[0 : lay.by], rows[lay.by :]
                    own[index, x, t] = jnp.where(core == 0, low, high)
                    theirs[index, x, t] = jnp.where(core == 0, high, low)
    else:
        z_out, y_out, d_out = refs[0], refs[1 : 1 + ny], refs[1 + ny : 1 + ny + nz * ny]
        for x in range(bx):
            store_packed(z_out, x, [latest[x, t] for t in range(zt)], lay, cy)
        for message, (high, _) in zip(y_out, y_sides):
            write_y_message(message, 0, y_rows_of(latest, lay, high), lay)
        corners = [(right, high) for right, _ in z_sides for high, _ in y_sides]
        for message, (right, high) in zip(d_out, corners):
            write_d_message(message, latest, lay, right, high)


def finish_kernel(lay, own, theirs, stored, image_before, *outs):
    src_prev, src_now, rec_prev, rec_now, snapshots, image = outs
    _, _, core = lay.place()
    first = core == 0
    for x in range(lay.bx):
        for t in range(lay.zt):
            width = LANES if t + 1 < lay.zt else lay.rest
            lanes = slice(t * LANES, t * LANES + width)
            source = [jnp.where(first, own[i, x, t], theirs[i, x, t])[:, :width] for i in range(lay.slots + 1)]
            receiver = [jnp.where(first, theirs[i, x, t], own[i, x, t])[:, :width] for i in range(lay.slots + 1)]
            src_prev[x, :, lanes], src_now[x, :, lanes] = source[0], source[1]
            rec_prev[x, :, lanes], rec_now[x, :, lanes] = receiver[0], receiver[1]
            total = image_before[x, :, lanes]
            for slot in range(lay.slots):
                kept = source[1] if slot == lay.slots - 1 else source[2 + slot]
                snapshots[slot, x, :, lanes] = kept.astype(jnp.bfloat16)
                crossed = receiver[1] if slot == 0 else receiver[1 + lay.slots - slot]
                total += stored[slot, x, :, lanes].astype(jnp.float32) * crossed
            image[x, :, lanes] = total


def call(kernel, outs, operands, scratch=(), scalars=0, aliases={}, from_hbm=False):
    in_specs = [pl.BlockSpec(memory_space=pltpu.SMEM)] * scalars
    space = pltpu.HBM if from_hbm else pltpu.VMEM
    if from_hbm:
        operands = [pltpu.with_memory_space_constraint(x, pltpu.HBM) for x in operands]
    in_specs += [pl.BlockSpec(memory_space=space)] * (len(operands) - scalars)
    return pl.pallas_call(
        kernel,
        out_shape=[jax.ShapeDtypeStruct(shape, dtype) for shape, dtype in outs],
        in_specs=in_specs,
        out_specs=[pl.BlockSpec(memory_space=pltpu.VMEM)] * len(outs),
        scratch_shapes=list(scratch),
        input_output_aliases=aliases,
        compiler_params=pltpu.CompilerParams(vmem_limit_bytes=6 * 1024 * 1024),
    )(*operands)


def share_in_chip(lay, message):
    other = lax.ppermute(message, AXES, lay.core_permutation())
    message = jnp.concatenate([message, other], 1)[None]
    if message.shape[2] != LANES:
        spare = -message.shape[2] % LANES
        fill = jnp.full((1, lay.trace_rows, spare), -1e6, jnp.float32)
        message = jnp.concatenate([message, fill], 2)
        message = message.reshape(lay.trace_rows, -1, LANES).transpose(1, 0, 2)
    return message


def spread(lay, message):
    for count, move in (
        (lay.columns, lambda x, c, bit: (x, c ^ bit)),
        (lay.nx, lambda x, c, bit: (x ^ bit, c)),
    ):
        assert count & (count - 1) == 0
        bit = 2
        while bit < count:
            pairs = lay.permutation(functools.partial(move, bit=bit))
            message = jnp.concatenate([message, lax.ppermute(message, AXES, pairs)], 0)
            bit *= 2
    return message


def body(
    mesh,
    source_prev,
    source_now,
    receiver_prev,
    receiver_now,
    speed_squared,
    wavelet,
    source_cell,
    traces,
    receiver_cells,
    plan,
    stored_snapshots,
    image_before,
):
    steps, slots = wavelet.shape[0], plan.shape[0]
    lay = Layout(mesh, *source_now.shape, steps, slots)
    f32 = jnp.float32
    first = lax.axis_index("gy") % 2 == 0
    nz, ny = len(lay.z_parities), len(lay.y_parities)

    half = (3, *source_now.shape)
    inputs = [source_now, source_prev, receiver_now, receiver_prev, speed_squared, traces, receiver_cells]
    mine, swapped, message = call(
        functools.partial(load_kernel, lay),
        [(half, f32), (half, f32), ((lay.trace_rows, traces.shape[1]), f32)],
        inputs,
        [
            pltpu.VMEM((4, *source_now.shape), f32),
            pltpu.VMEM(traces.shape, f32),
            pltpu.VMEM(receiver_cells.shape, jnp.int32),
            pltpu.SemaphoreType.DMA((8,)),
        ],
        from_hbm=True,
    )
    swapped = lax.ppermute(swapped, AXES, lay.core_permutation())
    groups = share_in_chip(lay, message)
    block = (lay.bx, lay.zt, lay.cy, LANES)
    ext = (lay.ex, lay.zt, lay.ey, LANES)
    field = (lay.bx + 2 * HALO, lay.zt, lay.cy + 2 * HALO, LANES)
    d_rows = lay.zt * ROWS
    y_rows = (2 * lay.zt - lay.packed) * ROWS
    z_shape = (lay.bx, lay.zrows, LANES)
    y_shape = (lay.bx // 2, y_rows, LANES)
    d_shape = (REACH // 2, d_rows, LANES)

    def carrying(planes, rows, first):
        more = pl.cdiv(groups.shape[0] * lay.trace_rows, rows) if first else 0
        return (planes + more, rows, LANES), f32

    outs = [(block, f32)] * 3
    outs += [carrying(lay.bx + 2 * REACH, lay.zrows, pz == 0) for pz in lay.z_parities]
    outs += [carrying(2 * (lay.bx // 2), y_rows, py == 0) for py in lay.y_parities]
    outs += [carrying(REACH // 2, d_rows, pz + py == 0) for pz in lay.z_parities for py in lay.y_parities]
    made = call(
        functools.partial(prepare_kernel, lay),
        outs,
        [mine, swapped, groups],
    )
    (p, q, s), made = made[:3], made[3:]
    z_out, y_out, d_out = made[:nz], made[nz : nz + ny], made[nz + ny :]

    for time in range(0, steps, 2):
        begin, end = time == 0, time + 2 == steps
        z_in = [lax.ppermute(m, AXES, lay.z_permutation(pz)) for m, pz in zip(z_out, lay.z_parities)]
        y_in = [lax.ppermute(m, AXES, lay.y_permutation(py)) for m, py in zip(y_out, lay.y_parities)]
        diagonals = [lay.d_permutation(pz, py) for pz in lay.z_parities for py in lay.y_parities]
        d_in = [lax.ppermute(m, AXES, pairs) for m, pairs in zip(d_out, diagonals)]
        if begin:
            d_in = list(lax.optimization_barrier(tuple(d_in)))
            carried = z_in[:1] + y_in[:1] + d_in[:1]
            (gathered,) = call(
                functools.partial(extract_kernel, lay),
                [((groups.shape[0] * (1 + len(carried)), *groups.shape[1:]), f32)],
                [source_cell, groups, *carried],
                scalars=1,
            )
            gathered = spread(lay, gathered)
        made = call(
            functools.partial(side_kernel, lay, time),
            [(ext, f32)] * (2 if begin else 1),
            [p, q, s, *z_in, *y_in],
            [pltpu.VMEM(ext, f32)] * begin + [pltpu.VMEM(field, f32)],
        )
        stepped = made[0]
        if begin:
            s = made[1]
            gathered, stepped = lax.optimization_barrier((gathered, stepped))
            (planes,) = call(
                functools.partial(planes_kernel, lay),
                [((lay.ex, lay.ey, LANES), f32)],
                [gathered],
                [pltpu.VMEM((lay.ex * lay.ey, LANES), f32)],
            )
        outs = [(ext, f32), ((steps, *block), f32)]
        if end:
            outs += [((slots + 1, lay.bx, lay.zt, lay.by, LANES), f32)] * 2
        else:
            outs += [(z_shape, f32)] + [(y_shape, f32)] * ny + [(d_shape, f32)] * (nz * ny)
        made = call(
            functools.partial(round_kernel, lay, time),
            outs,
            [source_cell, plan[None], wavelet[None], stepped, s, planes, p, *d_in],
            [pltpu.VMEM((REACH, lay.zt, 3 * ROWS, LANES), f32)],
            scalars=1,
            aliases={3: 0} | ({} if begin else {6: 1}),
        )
        q, p = made[:2]
        if end:
            own, theirs = made[2:]
        else:
            z_out = [made[2]] * nz
            y_out, d_out = made[3 : 3 + ny], made[3 + ny :]

    theirs = lax.ppermute(theirs, AXES, lay.core_permutation())
    shape = source_now.shape
    return tuple(
        call(
            functools.partial(finish_kernel, lay),
            [(shape, f32)] * 4 + [(stored_snapshots.shape, jnp.bfloat16), (shape, f32)],
            [own, theirs, stored_snapshots, image_before],
        )
    )


def solution(mesh):
    block = P(("shot", "gx"), "gy", None)
    line = P("shot", ("gx", "gy"))
    volume = P("shot", "gx", "gy", None)
    return jax.shard_map(
        functools.partial(body, mesh),
        mesh=mesh,
        in_specs=(block,) * 5 + (P("shot"), P("shot"), line, line, P("shot"), volume, block),
        out_specs=(block,) * 4 + (volume, block),
        check_vma=False,
    )
```

```python
import functools

import jax
import jax.numpy as jnp
from jax import lax
from jax.experimental import pallas as pl
from jax.experimental.pallas import tpu as pltpu
from jax.sharding import PartitionSpec as P

STENCIL_COEFFS = (-205.0 / 72.0, 8.0 / 5.0, -1.0 / 5.0, 8.0 / 315.0, -1.0 / 560.0)
REACH = 4
HALO = 2 * REACH
LANES = 128
ROWS = 8
AXES = ("gx", "gy")


class Layout:
    def __init__(self, mesh, block_x, block_y, depth, steps, slots):
        self.nx, self.ny = mesh.shape["gx"], mesh.shape["gy"]
        self.columns = self.ny // 2
        self.bx, self.by, self.depth = block_x, block_y, depth
        self.steps, self.slots = steps, slots
        self.cy = 2 * block_y
        self.zt = pl.cdiv(depth + REACH, LANES)
        self.rest = depth - (self.zt - 1) * LANES
        self.packed = 0 < self.rest <= LANES // 2
        self.ex, self.ey = block_x + 2 * REACH, self.cy + 2 * REACH
        self.zrows = self.cy * (self.zt - 1) + self.cy // 2 if self.packed else self.cy * self.zt
        self.trace_rows = pl.cdiv(steps + 2, 2 * ROWS) * 2 * ROWS
        self.z_parities = [p for p in (0, 1) if p + 1 < self.nx]
        self.y_parities = [p for p in (0, 1) if p + 1 < self.columns]
        assert self.ny % 2 == 0 and block_x >= HALO and block_x % 2 == 0 and block_y % ROWS == 0 and steps % 2 == 0

    def device(self, x, column, core):
        return x * self.ny + 2 * column + core

    def permutation(self, move):
        pairs = []
        for x in range(self.nx):
            for column in range(self.columns):
                other = move(x, column)
                there = 0 <= other[0] < self.nx and 0 <= other[1] < self.columns
                for core in (0, 1):
                    target = self.device(*other, core) if there else self.device(x, column, 1 - core)
                    pairs.append((self.device(x, column, core), target))
        return pairs

    def z_permutation(self, pz):
        return self.permutation(lambda x, c: (x + (1 if x % 2 == pz else -1), c))

    def y_permutation(self, py):
        return self.permutation(lambda x, c: (x, c + (1 if c % 2 == py else -1)))

    def d_permutation(self, pz, py):
        pairs = []
        for x in range(self.nx):
            for column in range(self.columns):
                beside = x + (1 if x % 2 == pz else -1)
                there = column + (1 if column % 2 == py else -1)
                for core in (0, 1):
                    if not 0 <= there < self.columns:
                        target = self.device(x, column, 1 - core)
                    else:
                        target = self.device(beside if 0 <= beside < self.nx else x, there, core)
                    pairs.append((self.device(x, column, core), target))
        return pairs

    def carriers(self, z_messages, y_messages, d_messages):
        starts = (self.bx + 2 * REACH, 2 * (self.bx // 2), REACH // 2)
        return [(m, start) for ms, start in zip((z_messages, y_messages, d_messages), starts) for m in ms]

    def by_kind(self, messages):
        z, y = bool(self.z_parities), bool(self.y_parities)
        return messages[:z], messages[z : z + y], messages[z + y :]

    def spot(self, message, start, group, part):
        chunk = group * (self.trace_rows // ROWS) + part
        per_plane = message.shape[1] // ROWS
        return start + chunk // per_plane, chunk % per_plane * ROWS

    def core_permutation(self):
        return self.permutation(lambda x, c: (-1, -1))

    def place(self):
        gx, gy = lax.axis_index("gx"), lax.axis_index("gy")
        return gx, gy // 2, gy % 2

    def z_side(self, pz):
        gx, _, _ = self.place()
        right = gx % 2 == pz
        return right, jnp.where(right, gx + 1 < self.nx, gx > 0)

    def y_side(self, py):
        _, column, _ = self.place()
        high = column % 2 == py
        return high, jnp.where(high, column + 1 < self.columns, column > 0)


def lane_ids(rows):
    return lax.broadcasted_iota(jnp.int32, (rows, LANES), 1)


def pack(tiles, lay, rows):
    if not lay.packed:
        return list(tiles)
    last = tiles[-1]
    return list(tiles[:-1]) + [last[: rows // 2] + pltpu.roll(last[rows // 2 :], LANES // 2, 1)]


def unpack(block, lay, rows):
    tiles = [block[t * rows : (t + 1) * rows] for t in range(lay.zt - 1)]
    start = (lay.zt - 1) * rows
    if not lay.packed:
        return tiles + [block[start : start + rows]]
    both = block[start : start + rows // 2]
    low = lane_ids(rows // 2) < LANES // 2
    first = jnp.where(low, both, 0.0)
    second = pltpu.roll(jnp.where(low, 0.0, both), LANES // 2, 1)
    return tiles + [jnp.concatenate([first, second], 0)]


def store_packed(ref, index, tiles, lay, rows):
    row = 0
    for piece in pack(tiles, lay, rows):
        ref[index, row : row + piece.shape[0], :] = piece
        row += piece.shape[0]


def y_rows_of(source, lay, high):
    def rows(plane, t):
        return jnp.where(high, source[plane, t, lay.cy - ROWS : lay.cy, :], source[plane, t, 0:ROWS, :])

    return rows


def y_halves_of(first, second, lay, high):
    upper = lax.broadcasted_iota(jnp.int32, (ROWS, LANES), 0) < REACH
    a, b = y_rows_of(first, lay, high), y_rows_of(second, lay, high)

    def rows(plane, t):
        one, two = a(plane, t), b(plane, t)
        one = jnp.where(high, pltpu.roll(one, REACH, 0), one)
        two = jnp.where(high, two, pltpu.roll(two, REACH, 0))
        return jnp.where(upper, one, two)

    return rows


def write_y_message(ref, lead, rows_of, lay):
    half = lay.bx // 2
    for x in range(half):
        row = 0
        for t in range(lay.zt):
            a, b = rows_of(x, t), rows_of(x + half, t)
            both = [a + pltpu.roll(b, LANES // 2, 1)] if lay.packed and t + 1 == lay.zt else [a, b]
            for rows in both:
                ref[lead * half + x, row : row + ROWS, :] = rows
                row += ROWS


def read_y_message(ref, lead, lay, x, t):
    half = lay.bx // 2
    plane, second = lead * half + x % half, x >= half
    row = 2 * t * ROWS
    if not lay.packed or t + 1 < lay.zt:
        row += ROWS * second
        return ref[plane, row : row + ROWS, :]
    both = ref[plane, row : row + ROWS, :]
    low = lane_ids(ROWS) < LANES // 2
    return pltpu.roll(jnp.where(low, 0.0, both), LANES // 2, 1) if second else jnp.where(low, both, 0.0)


def write_d_message(ref, source, lay, right, high):
    start = jnp.where(right, lay.bx - REACH, 0)
    upper = lax.broadcasted_iota(jnp.int32, (ROWS, LANES), 0) < REACH
    for x in range(REACH // 2):
        for t in range(lay.zt):
            a, b = (
                jnp.where(
                    high,
                    source[start + plane, t, lay.cy - ROWS : lay.cy, :],
                    source[start + plane, t, 0:ROWS, :],
                )
                for plane in (x, x + REACH // 2)
            )
            last = jnp.where(upper, pltpu.roll(a, REACH, 0), b)
            first = jnp.where(upper, a, pltpu.roll(b, REACH, 0))
            ref[x, t * ROWS : (t + 1) * ROWS, :] = jnp.where(high, last, first)


def load_kernel(lay, src_now, src_prev, rec_now, rec_prev, speed, traces, cells, mine, swap, message, *scratch):
    held, samples, numbers, semaphores = scratch
    copies = [
        (src_now, held.at[0]),
        (rec_now, held.at[1]),
        (src_prev, held.at[2]),
        (rec_prev, held.at[3]),
        (speed, mine.at[2]),
        (speed, swap.at[2]),
        (traces, samples),
        (cells, numbers),
    ]
    copies = [pltpu.make_async_copy(a, b, semaphores.at[i]) for i, (a, b) in enumerate(copies)]
    for copy in copies:
        copy.start()
    for copy in copies:
        copy.wait()
    _, _, core = lay.place()
    for index in range(2):
        for x in range(lay.bx):
            source, receiver = held[2 * index, x], held[2 * index + 1, x]
            mine[index, x] = jnp.where(core == 0, source, receiver)
            swap[index, x] = jnp.where(core == 0, receiver, source)
    cell = numbers[...].astype(jnp.float32)
    row = jnp.floor((cell + 0.5) * (1.0 / (lay.by * lay.ny)))
    message[...] = jnp.zeros_like(message)
    message[0 : lay.steps, :] = samples[...]
    message[lay.steps : lay.steps + 1, :] = row
    message[lay.steps + 1 : lay.steps + 2, :] = cell - row * (lay.by * lay.ny)


def prepare_kernel(lay, *refs):
    (own, other, groups), refs = refs[:3], refs[3:]
    (p, q, s), refs = refs[:3], refs[3:]
    nz, ny = len(lay.z_parities), len(lay.y_parities)
    z_messages, refs = refs[:nz], refs[nz:]
    y_messages, d_messages = refs[:ny], refs[ny:]
    _, _, core = lay.place()
    first = core == 0
    edge = (lay.zt - 1) * LANES
    for ref in (p, q, s):
        ref[:, lay.zt - 1, :, :] = jnp.zeros((lay.bx, lay.cy, LANES), jnp.float32)
    for index, ref in enumerate((p, q, s)):
        for x in range(lay.bx):
            for t in range(lay.zt):
                width = LANES if t + 1 < lay.zt else lay.rest
                lanes = slice(t * LANES, t * LANES + width)
                mine = own[index, x, :, lanes]
                theirs = other[index, x, :, lanes]
                ref[x, t, 0 : lay.by, 0:width] = jnp.where(first, mine, theirs)
                ref[x, t, lay.by : lay.cy, 0:width] = jnp.where(first, theirs, mine)
    sides = [lay.z_side(pz)[0] for pz in lay.z_parities]
    for x in range(lay.bx):
        tiles = [p[x, t] for t in range(lay.zt)]
        for message in z_messages:
            store_packed(message, x, tiles, lay, lay.cy)
    for message, right in zip(z_messages, sides):
        start = jnp.where(right, lay.bx - REACH, 0)
        for lead, ref in ((0, q), (1, s)):
            for x in range(REACH):
                tiles = [ref[start + x, t] for t in range(lay.zt)]
                store_packed(message, lay.bx + lead * REACH + x, tiles, lay, lay.cy)
    highs = [lay.y_side(py)[0] for py in lay.y_parities]
    for message, high in zip(y_messages, highs):
        write_y_message(message, 0, y_rows_of(p, lay, high), lay)
        write_y_message(message, 1, y_halves_of(q, s, lay, high), lay)
    corners = [(right, high) for right in sides for high in highs]
    for message, (right, high) in zip(d_messages, corners):
        write_d_message(message, p, lay, right, high)
    for message, start in lay.carriers(z_messages[:1], y_messages[:1], d_messages[:1]):
        for group in range(groups.shape[0]):
            for part in range(lay.trace_rows // ROWS):
                plane, row = lay.spot(message, start, group, part)
                message[plane, row : row + ROWS, :] = groups[group, part * ROWS : (part + 1) * ROWS, :]


def extract_kernel(lay, *refs):
    groups, messages, out = refs[1], refs[2:-1], refs[-1]
    count = groups.shape[0]
    out[0:count] = groups[...]
    for index, (message, start) in enumerate(lay.carriers(*lay.by_kind(messages))):
        for group in range(count):
            for part in range(lay.trace_rows // ROWS):
                plane, row = lay.spot(message, start, group, part)
                out[(index + 1) * count + group, part * ROWS : (part + 1) * ROWS, :] = message[plane, row : row + ROWS, :]


def planes_kernel(lay, groups, planes, total):
    gx, column, core = lay.place()
    start_x, start_y = gx * lay.bx - REACH, column * lay.cy - REACH
    cells = lay.ex * lay.ey
    padded = lay.trace_rows
    total[...] = jnp.zeros_like(total)

    def add(values):
        x = values[lay.steps : lay.steps + 1, :].astype(jnp.int32) - start_x
        y = values[lay.steps + 1 : lay.steps + 2, :].astype(jnp.int32) - start_y
        inside = (x >= 0) & (x < lay.ex) & (y >= 0) & (y < lay.ey)
        cell = jnp.where(inside, x * lay.ey + y, -1)
        ids = lax.broadcasted_iota(jnp.int32, (cells, LANES), 0)
        chosen = jnp.where(ids == cell, 1.0, 0.0).astype(jnp.bfloat16)
        high = values.astype(jnp.bfloat16)
        rest = values - high.astype(jnp.float32)
        middle = rest.astype(jnp.bfloat16)
        low = (rest - middle.astype(jnp.float32)).astype(jnp.bfloat16)
        fill = jnp.zeros((LANES - 3 * padded, LANES), jnp.bfloat16)
        parts = jnp.concatenate([high, middle, low, fill], 0)
        total[...] += lax.dot_general(
            chosen, parts, (((1,), (1,)), ((), ())), preferred_element_type=jnp.float32
        )

    def add_group(group, carry):
        add(groups[group])
        return carry

    lax.fori_loop(0, groups.shape[0], add_group, 0, unroll=groups.shape[0] <= 2 * ROWS)
    summed = total[...]
    summed = (
        summed + pltpu.roll(summed, LANES - padded, 1) + pltpu.roll(summed, LANES - 2 * padded, 1)
    )
    summed = jnp.where(core == 1, summed, 0.0)
    planes[...] = summed.reshape(lay.ex, lay.ey, LANES)


def advance(lay, field, x, y, rows, before, speed):
    lane = lane_ids(rows)
    centre = [field[x, t, y : y + rows, :] for t in range(lay.zt)]
    sums = []
    for k in range(1, REACH + 1):
        left = [pltpu.roll(c, k, 1) for c in centre]
        right = [pltpu.roll(c, LANES - k, 1) for c in centre]
        per_tile = []
        for t in range(lay.zt):
            lower = jnp.where(lane < k, left[t - 1], left[t])
            upper = jnp.where(lane < LANES - k, right[t], right[(t + 1) % lay.zt])
            around = field[x - k, t, y : y + rows, :] + field[x + k, t, y : y + rows, :]
            around += field[x, t, y - k : y - k + rows, :] + field[x, t, y + k : y + k + rows, :]
            per_tile.append(around + (lower + upper))
        sums.append(per_tile)
    out = []
    for t in range(lay.zt):
        drive = 3.0 * STENCIL_COEFFS[0] * centre[t]
        for k in range(REACH):
            drive += STENCIL_COEFFS[k + 1] * sums[k][t]
        out.append(2.0 * centre[t] - before[t] + speed[t] * drive)
    return out


def side_kernel(lay, time, *refs):
    nz, ny = len(lay.z_parities), len(lay.y_parities)
    (p, q, s), refs = refs[:3], refs[3:]
    first = time == 0
    if not first:
        p = p.at[time - 1]
    z_in, refs = refs[:nz], refs[nz:]
    y_in, refs = refs[:ny], refs[ny:]
    refs = refs if first else refs[1:]
    stepped, buffer = refs[0], refs[-1]
    meet = refs[2] if first else refs[1]
    meet[...] = jnp.zeros_like(meet)
    z_sides = [lay.z_side(pz) for pz in lay.z_parities]
    y_sides = [lay.y_side(py) for py in lay.y_parities]
    bx, cy, zt = lay.bx, lay.cy, lay.zt
    own_x, own_y = HALO, HALO

    buffer[own_x : own_x + bx, :, own_y : own_y + cy, :] = p[...]
    around = ((own_x - REACH, own_x), (own_x + bx, own_x + bx + REACH))
    for low, high in around if ny == 2 else ((own_x - REACH, own_x + bx + REACH),):
        empty = jnp.zeros((high - low, zt, HALO, LANES), jnp.float32)
        buffer[low:high, :, 0:own_y, :] = empty
        buffer[low:high, :, own_y + cy :, :] = empty
    if nz < 2:
        empty = jnp.zeros((own_x, zt, cy, LANES), jnp.float32)
        buffer[0:own_x, :, own_y : own_y + cy, :] = empty
        buffer[own_x + bx :, :, own_y : own_y + cy, :] = empty
    for (right, valid), message in zip(z_sides, z_in):
        start = jnp.where(right, own_x + bx, 0)
        skip = jnp.where(right, 0, bx - HALO)
        for x in range(HALO):
            block = jnp.where(valid, message[skip + x], 0.0)
            for t, tile in enumerate(unpack(block, lay, cy)):
                buffer[start + x, t, own_y : own_y + cy, :] = tile
    for (high, valid), message in zip(y_sides, y_in):
        start = pl.multiple_of(jnp.where(high, own_y + cy, own_y - ROWS), ROWS)
        for x in range(bx):
            for t in range(zt):
                rows = read_y_message(message, 0, lay, x, t)
                buffer[own_x + x, t, pl.ds(start, ROWS), :] = jnp.where(valid, rows, 0.0)

    if first:
        s_out, q_ext = refs[1], refs[3]
        for lead, own, ext in ((0, q, q_ext), (1, s, s_out)):
            ext[...] = jnp.zeros_like(ext)
            for x in range(bx):
                for t in range(zt):
                    ext[REACH + x, t, REACH : REACH + cy, :] = own[x, t]
            for (right, valid), message in zip(z_sides, z_in):
                start = jnp.where(right, REACH + bx, 0)
                for x in range(REACH):
                    block = jnp.where(valid, message[bx + lead * REACH + x], 0.0)
                    for t, tile in enumerate(unpack(block, lay, cy)):
                        ext[start + x, t, REACH : REACH + cy, :] = tile
            cut = lead * REACH
            for is_high, start in ((False, 0), (True, REACH + cy)):
                wants = [v & (h if is_high else ~h) for h, v in y_sides]
                for x in range(bx):
                    for t in range(zt):
                        rows = sum(
                            (jnp.where(w, read_y_message(m, 1, lay, x, t), 0.0) for w, m in zip(wants, y_in)),
                            jnp.zeros((ROWS, LANES), jnp.float32),
                        )
                        ext[REACH + x, t, start : start + REACH, :] = rows[cut : cut + REACH]
        q, s = q_ext, s_out

    for x in range(lay.ex):
        inside = REACH <= x < REACH + bx
        y, count = (0, lay.ey) if inside else (REACH, cy)
        out = advance(
            lay, buffer, x + REACH, y + REACH, count,
            [q[x, t, y : y + count, :] for t in range(zt)],
            [s[x, t, y : y + count, :] for t in range(zt)],
        )
        for t in range(zt):
            stepped[x, t, y : y + count, :] = out[t]


def add_corner(lay, field, s, message, right, high, valid, corner):
    empty = jnp.zeros((REACH, lay.zt, ROWS, LANES), jnp.float32)
    corner[:, :, 0:ROWS, :] = empty
    corner[:, :, 2 * ROWS :, :] = empty
    upper = lax.broadcasted_iota(jnp.int32, (ROWS, LANES), 0) < REACH
    near = jnp.where(upper, 1.0, 0.0)
    keep = jnp.where(valid, jnp.where(high, near, 1.0 - near), 0.0)
    for x in range(REACH // 2):
        for t in range(lay.zt):
            rows = message[x, t * ROWS : (t + 1) * ROWS, :]
            turned = pltpu.roll(rows, REACH, 0)
            corner[x, t, ROWS : 2 * ROWS, :] = jnp.where(high, rows, turned) * keep
            corner[x + REACH // 2, t, ROWS : 2 * ROWS, :] = jnp.where(high, turned, rows) * keep
    planes_start = jnp.where(right, REACH + lay.bx, 0)
    rows_start = jnp.where(right, lay.bx, REACH)

    def add(is_high):
        near = REACH + lay.cy - ROWS if is_high else REACH
        edge, cut = (lay.ey - ROWS, REACH) if is_high else (0, 2 * ROWS - REACH)
        for t in range(lay.zt):
            source = [corner[j, t, cut : cut + ROWS, :] for j in range(REACH)]
            for x in range(REACH):
                amount = sum(
                    STENCIL_COEFFS[k] * corner[x, t, pl.ds(k if is_high else 2 * ROWS - k, ROWS), :]
                    for k in range(1, REACH + 1)
                )
                rows = slice(near, near + ROWS)
                field[planes_start + x, t, rows, :] += s[planes_start + x, t, rows, :] * amount
                from_left = sum(STENCIL_COEFFS[x + REACH - j] * source[j] for j in range(x, REACH))
                from_right = sum(STENCIL_COEFFS[REACH + j - x] * source[j] for j in range(x + 1))
                amount = jnp.where(right, from_right, from_left)
                rows = slice(edge, edge + ROWS)
                field[rows_start + x, t, rows, :] += s[rows_start + x, t, rows, :] * amount

    pl.when(high)(functools.partial(add, True))
    pl.when(jnp.logical_not(high))(functools.partial(add, False))


def round_kernel(lay, time, *refs):
    nz, ny = len(lay.z_parities), len(lay.y_parities)
    last = time + 2 == lay.steps
    (source_cell, plan, wavelet, stepped, s, planes, p), refs = refs[:7], refs[7:]
    d_in, refs = refs[: nz * ny], refs[nz * ny :]
    (field, history), refs = refs[:2], refs[2:]
    corner = refs[-1]
    latest = history.at[time + 1]
    if time:
        p = history.at[time - 1]
    gx, column, core = lay.place()
    cell, grid_y = source_cell[0], lay.by * lay.ny
    source_x = cell // (grid_y * lay.depth) - gx * lay.bx
    source_y = cell // lay.depth % grid_y - column * lay.cy
    source_z = cell % lay.depth
    z_sides = [lay.z_side(pz) for pz in lay.z_parities]
    y_sides = [lay.y_side(py) for py in lay.y_parities]
    bx, cy, zt = lay.bx, lay.cy, lay.zt

    def injected(x, rows, y, back):
        values = pltpu.roll(planes[x], LANES - back, 1) if back else planes[x]
        return jnp.where(lane_ids(lay.ey) == 0, values, 0.0)[y : y + rows]

    def add_source(target, speed_rows, x, y, count_x, count_y, amount):
        @pl.when((core == 0) & (x >= 0) & (x < count_x) & (y >= 0) & (y < count_y))
        def _():
            tile, lane = source_z // LANES, source_z % LANES
            shape = (count_y, LANES)
            here = (lax.broadcasted_iota(jnp.int32, shape, 0) == y) & (
                lax.broadcasted_iota(jnp.int32, shape, 1) == lane
            )
            target[x, tile] += jnp.where(here, speed_rows(x, tile) * amount, 0.0)

    corners = [(r, h, u & v) for r, u in z_sides for h, v in y_sides]
    for (right, high, valid), message in zip(corners, d_in):
        add_corner(lay, field, s, message, right, high, valid, corner)
    for x in range(lay.ex):
        field[x, 0] += s[x, 0] * injected(x, lay.ey, 0, lay.steps - 1 - time)
    add_source(field, lambda x, t: s[x, t], source_x + REACH, source_y + REACH, lay.ex, lay.ey, wavelet[:, time : time + 1])

    for x in range(bx):
        speed = [s[x + REACH, t, REACH : REACH + cy, :] for t in range(zt)]
        out = advance(lay, field, x + REACH, REACH, cy, [p[x, t] for t in range(zt)], speed)
        out[0] += speed[0] * injected(x + REACH, cy, REACH, lay.steps - 2 - time)
        for t in range(zt):
            latest[x, t] = out[t]
            history[time, x, t] = field[x + REACH, t, REACH : REACH + cy, :]
    add_source(
        latest, lambda x, t: s[x + REACH, t, REACH : REACH + cy, :], source_x, source_y, bx, cy, wavelet[:, time + 1 : time + 2]
    )

    if last:
        own, theirs = refs[:2]

        def kept(index, x, t):
            if index < 3:
                return history[(lay.steps - 2, lay.steps - 1, 0)[index], x, t]
            slot = index - 2
            rows = history[slot, x, t]
            for moment in range(slot + 1, lay.steps - lay.slots + slot + 1):
                rows = jnp.where(moments[slot] == moment, history[moment, x, t], rows)
            return rows

        moments = {}
        for slot in range(1, lay.slots - 1):
            mirrored = lay.slots - 1 - slot
            moment = jnp.where(core == 0, plan[:, slot : slot + 1], lay.steps - 1 - plan[:, mirrored : mirrored + 1])
            moments[slot] = jnp.broadcast_to(moment, (cy, LANES))
        for index in range(lay.slots + 1):
            for x in range(bx):
                for t in range(zt):
                    rows = kept(index, x, t)
                    low, high = rows[0 : lay.by], rows[lay.by :]
                    own[index, x, t] = jnp.where(core == 0, low, high)
                    theirs[index, x, t] = jnp.where(core == 0, high, low)
    else:
        z_out, y_out, d_out = refs[0], refs[1 : 1 + ny], refs[1 + ny : 1 + ny + nz * ny]
        for x in range(bx):
            store_packed(z_out, x, [latest[x, t] for t in range(zt)], lay, cy)
        for message, (high, _) in zip(y_out, y_sides):
            write_y_message(message, 0, y_rows_of(latest, lay, high), lay)
        corners = [(right, high) for right, _ in z_sides for high, _ in y_sides]
        for message, (right, high) in zip(d_out, corners):
            write_d_message(message, latest, lay, right, high)


def finish_kernel(lay, own, theirs, stored, image_before, *outs):
    src_prev, src_now, rec_prev, rec_now, snapshots, image = outs
    _, _, core = lay.place()
    first = core == 0
    for x in range(lay.bx):
        for t in range(lay.zt):
            width = LANES if t + 1 < lay.zt else lay.rest
            lanes = slice(t * LANES, t * LANES + width)
            source = [jnp.where(first, own[i, x, t], theirs[i, x, t])[:, :width] for i in range(lay.slots + 1)]
            receiver = [jnp.where(first, theirs[i, x, t], own[i, x, t])[:, :width] for i in range(lay.slots + 1)]
            src_prev[x, :, lanes], src_now[x, :, lanes] = source[0], source[1]
            rec_prev[x, :, lanes], rec_now[x, :, lanes] = receiver[0], receiver[1]
            total = image_before[x, :, lanes]
            for slot in range(lay.slots):
                kept = source[1] if slot == lay.slots - 1 else source[2 + slot]
                snapshots[slot, x, :, lanes] = kept.astype(jnp.bfloat16)
                crossed = receiver[1] if slot == 0 else receiver[1 + lay.slots - slot]
                total += stored[slot, x, :, lanes].astype(jnp.float32) * crossed
            image[x, :, lanes] = total


def call(kernel, outs, operands, scratch=(), scalars=0, aliases={}, from_hbm=False):
    in_specs = [pl.BlockSpec(memory_space=pltpu.SMEM)] * scalars
    space = pltpu.HBM if from_hbm else pltpu.VMEM
    if from_hbm:
        operands = [pltpu.with_memory_space_constraint(x, pltpu.HBM) for x in operands]
    in_specs += [pl.BlockSpec(memory_space=space)] * (len(operands) - scalars)
    return pl.pallas_call(
        kernel,
        out_shape=[jax.ShapeDtypeStruct(shape, dtype) for shape, dtype in outs],
        in_specs=in_specs,
        out_specs=[pl.BlockSpec(memory_space=pltpu.VMEM)] * len(outs),
        scratch_shapes=list(scratch),
        input_output_aliases=aliases,
        compiler_params=pltpu.CompilerParams(vmem_limit_bytes=6 * 1024 * 1024),
    )(*operands)


def share_in_chip(lay, message):
    other = lax.ppermute(message, AXES, lay.core_permutation())
    message = jnp.concatenate([message, other], 1)[None]
    if message.shape[2] != LANES:
        spare = -message.shape[2] % LANES
        fill = jnp.full((1, lay.trace_rows, spare), -1e6, jnp.float32)
        message = jnp.concatenate([message, fill], 2)
        message = message.reshape(lay.trace_rows, -1, LANES).transpose(1, 0, 2)
    return message


def spread(lay, message):
    for count, move in (
        (lay.columns, lambda x, c, bit: (x, c ^ bit)),
        (lay.nx, lambda x, c, bit: (x ^ bit, c)),
    ):
        assert count & (count - 1) == 0
        bit = 2
        while bit < count:
            pairs = lay.permutation(functools.partial(move, bit=bit))
            message = jnp.concatenate([message, lax.ppermute(message, AXES, pairs)], 0)
            bit *= 2
    return message


def body(
    mesh,
    source_prev,
    source_now,
    receiver_prev,
    receiver_now,
    speed_squared,
    wavelet,
    source_cell,
    traces,
    receiver_cells,
    plan,
    stored_snapshots,
    image_before,
):
    steps, slots = wavelet.shape[0], plan.shape[0]
    lay = Layout(mesh, *source_now.shape, steps, slots)
    f32 = jnp.float32
    first = lax.axis_index("gy") % 2 == 0
    nz, ny = len(lay.z_parities), len(lay.y_parities)

    half = (3, *source_now.shape)
    inputs = [source_now, source_prev, receiver_now, receiver_prev, speed_squared, traces, receiver_cells]
    mine, swapped, message = call(
        functools.partial(load_kernel, lay),
        [(half, f32), (half, f32), ((lay.trace_rows, traces.shape[1]), f32)],
        inputs,
        [
            pltpu.VMEM((4, *source_now.shape), f32),
            pltpu.VMEM(traces.shape, f32),
            pltpu.VMEM(receiver_cells.shape, jnp.int32),
            pltpu.SemaphoreType.DMA((8,)),
        ],
        from_hbm=True,
    )
    swapped = lax.ppermute(swapped, AXES, lay.core_permutation())
    groups = share_in_chip(lay, message)
    block = (lay.bx, lay.zt, lay.cy, LANES)
    ext = (lay.ex, lay.zt, lay.ey, LANES)
    field = (lay.bx + 2 * HALO, lay.zt, lay.cy + 2 * HALO, LANES)
    d_rows = lay.zt * ROWS
    y_rows = (2 * lay.zt - lay.packed) * ROWS
    z_shape = (lay.bx, lay.zrows, LANES)
    y_shape = (lay.bx // 2, y_rows, LANES)
    d_shape = (REACH // 2, d_rows, LANES)

    def carrying(planes, rows, first):
        more = pl.cdiv(groups.shape[0] * lay.trace_rows, rows) if first else 0
        return (planes + more, rows, LANES), f32

    outs = [(block, f32)] * 3
    outs += [carrying(lay.bx + 2 * REACH, lay.zrows, pz == 0) for pz in lay.z_parities]
    outs += [carrying(2 * (lay.bx // 2), y_rows, py == 0) for py in lay.y_parities]
    outs += [carrying(REACH // 2, d_rows, pz + py == 0) for pz in lay.z_parities for py in lay.y_parities]
    made = call(
        functools.partial(prepare_kernel, lay),
        outs,
        [mine, swapped, groups],
    )
    (p, q, s), made = made[:3], made[3:]
    z_out, y_out, d_out = made[:nz], made[nz : nz + ny], made[nz + ny :]

    met = []
    for time in range(0, steps, 2):
        begin, end = time == 0, time + 2 == steps
        z_in = [lax.ppermute(m, AXES, lay.z_permutation(pz)) for m, pz in zip(z_out, lay.z_parities)]
        y_in = [lax.ppermute(m, AXES, lay.y_permutation(py)) for m, py in zip(y_out, lay.y_parities)]
        diagonals = [lay.d_permutation(pz, py) for pz in lay.z_parities for py in lay.y_parities]
        d_in = [lax.ppermute(m, AXES, pairs) for m, pairs in zip(d_out, diagonals)]
        if begin:
            d_in = list(lax.optimization_barrier(tuple(d_in)))
            carried = z_in[:1] + y_in[:1] + d_in[:1]
            (gathered,) = call(
                functools.partial(extract_kernel, lay),
                [((groups.shape[0] * (1 + len(carried)), *groups.shape[1:]), f32)],
                [source_cell, groups, *carried],
                scalars=1,
            )
            gathered = spread(lay, gathered)
        made = call(
            functools.partial(side_kernel, lay, time),
            [(ext, f32)] * (2 if begin else 1) + [((ROWS, LANES), f32)],
            [p, q, s, *z_in, *y_in, *met],
            [pltpu.VMEM(ext, f32)] * begin + [pltpu.VMEM(field, f32)],
        )
        stepped = made[0]
        met = [lax.ppermute(made[-1], AXES, lay.core_permutation())]
        if begin:
            s = made[1]
            gathered, stepped = lax.optimization_barrier((gathered, stepped))
            (planes,) = call(
                functools.partial(planes_kernel, lay),
                [((lay.ex, lay.ey, LANES), f32)],
                [gathered],
                [pltpu.VMEM((lay.ex * lay.ey, LANES), f32)],
            )
        outs = [(ext, f32), ((steps, *block), f32)]
        if end:
            outs += [((slots + 1, lay.bx, lay.zt, lay.by, LANES), f32)] * 2
        else:
            outs += [(z_shape, f32)] + [(y_shape, f32)] * ny + [(d_shape, f32)] * (nz * ny)
        made = call(
            functools.partial(round_kernel, lay, time),
            outs,
            [source_cell, plan[None], wavelet[None], stepped, s, planes, p, *d_in],
            [pltpu.VMEM((REACH, lay.zt, 3 * ROWS, LANES), f32)],
            scalars=1,
            aliases={3: 0} | ({} if begin else {6: 1}),
        )
        q, p = made[:2]
        if end:
            own, theirs = made[2:]
        else:
            packed, met[0] = lax.optimization_barrier((made[2], met[0]))
            z_out = [packed] * nz
            y_out, d_out = made[3 : 3 + ny], made[3 + ny :]

    theirs = lax.ppermute(theirs, AXES, lay.core_permutation())
    shape = source_now.shape
    return tuple(
        call(
            functools.partial(finish_kernel, lay),
            [(shape, f32)] * 4 + [(stored_snapshots.shape, jnp.bfloat16), (shape, f32)],
            [own, theirs, stored_snapshots, image_before],
        )
    )


def solution(mesh):
    block = P(("shot", "gx"), "gy", None)
    line = P("shot", ("gx", "gy"))
    volume = P("shot", "gx", "gy", None)
    return jax.shard_map(
        functools.partial(body, mesh),
        mesh=mesh,
        in_specs=(block,) * 5 + (P("shot"), P("shot"), line, line, P("shot"), volume, block),
        out_specs=(block,) * 4 + (volume, block),
        check_vma=False,
    )
```
